128 devices in a mesh: group: 32 (over y, z, core), tensor: 4 (over x).
Axes of the slice: x: 4, y: 4, z: 4, core: 2. Of those that a mesh axis runs over, the one named last changes fastest.
Arguments:
- queries: bfloat16 [4096, 8192], P('group', 'tensor'), may hold values from -256 to 256
- hidden_rows: bfloat16 [4096, 8192], P(('group', 'tensor')), may hold values from -6 to 6
- kv_weight: bfloat16 [2, 8192, 1024], P(None, None, 'tensor'), may hold values from -0.0625 to 0.0625
- cache_keys: bfloat16 [4096, 1024], P('group', 'tensor'), may hold values from -8 to 8
- cache_values: bfloat16 [4096, 1024], P('group', 'tensor'), may hold values from -6 to 6
- kv_blocks: int32 [32], replicated, may hold values from 1 to 4, 64 in all
Outputs:
- attended: bfloat16 [4096, 8192], P('group', 'tensor')
- new_keys: bfloat16 [4096, 1024], P('group', 'tensor')
- new_values: bfloat16 [4096, 1024], P('group', 'tensor')
The draws below stay inside these ranges and needn't reach their ends.
Inputs may be any that keep to these rules, and one draw needn't show every extreme that they name: `kv_blocks`: they sum to 32 * 4 // 2 over the groups, and some group has 4.
All inputs are finite; a program needn't handle non-finite values.
Results may differ from the reference program's by a relative error of at most 0.009.
Values may be sent and summed in bfloat16 or wider, within the bound.
No kernel may reach another device: no remote copies, remote signals or barrier semaphores. Data moves between devices by JAX's collectives and lax.ppermute only.
A program may use at most 64 MiB of HBM per device.

```python
import math
import jax
import jax.numpy as jnp
import numpy as np
from jax import lax

D = 8192
HEADS = 64
KV_HEADS = 8
HEAD_DIM = 128
NEW_ROWS = 128
BLOCK = 32
NBLK = 4
PREFIX_CAP = 128
SEGMENT = 4096
KVD = 1024
QD = 8192
N_GROUP = 32


def key_field(key):
    base = jax.random.normal(jax.random.fold_in(key, 11), (N_GROUP * PREFIX_CAP, KVD), jnp.float32)
    return jnp.clip(base, -6.0, 6.0)


def draw_cache_keys(key, part):
    field = key_field(key)
    return field.astype(jnp.bfloat16)


def draw_queries(key, part):
    own_key = jax.random.fold_in(key, 5)
    base = 2.5 * jnp.clip(jax.random.normal(own_key, (SEGMENT, QD), jnp.float32), -6.0, 6.0)
    return base.astype(jnp.bfloat16)


def block_levels(rng, extent, cuts, least, top_value):
    level = 1.0
    for dim, parts in cuts:
        draws = jax.random.uniform(jax.random.fold_in(jax.random.fold_in(rng, 6), dim), (parts,), jnp.float32, least / len(cuts), top_value / len(cuts))
        level = level * jnp.repeat(jnp.exp(draws), extent[dim] // parts).reshape((-1,) + (1,) * (len(extent) - 1 - dim))
    return level


def length_profile(amount, total, bound, slope):
    weights = [(1 << 20) // math.isqrt(rank ** slope) + 1 for rank in range(2, amount + 1)]
    spare, counts = total - bound - (amount - 1), [1] * (amount - 1)
    while spare > 0:
        free = [i for i in range(amount - 1) if counts[i] < bound]
        pool, budget = sum([weights[i] for i in free]), spare
        for i in free:
            addition = min(bound - counts[i], max(1, budget * weights[i] // pool), spare)
            counts[i] = counts[i] + addition
            spare = spare - addition
    return np.array([bound] + counts)


def uneven_parts(stream_key, count, total, most, lean):
    if count == 2:
        one = jax.random.randint(stream_key, (), max(1, total - most), min(most, total - 1) + 1)
        return jnp.stack([one, total - one])
    lengths = jnp.asarray(length_profile(count, total, most, lean), jnp.int32)
    twos = (count - 1) // 2
    giver, sink = lengths[1:1 + 2 * twos:2], lengths[2:2 + 2 * twos:2]
    slack = jnp.minimum(giver - 1, most - sink)
    passed = jax.random.randint(jax.random.fold_in(stream_key, 1), (twos,), 0, 1 << 20) % (slack + 1)
    lengths = lengths.at[1:1 + 2 * twos:2].set(giver - passed).at[2:2 + 2 * twos:2].set(sink + passed)
    return lengths[jax.random.permutation(jax.random.fold_in(stream_key, 2), count)]


def scatter_about(key, extent, width, reach, shards=(), held_as=jnp.bfloat16):
    gain = block_levels(key, extent, shards, -0.22, 0.18) if shards else 1.0
    values = jax.random.normal(key, extent, jnp.float32) * width * gain
    return jnp.minimum(jnp.maximum(values, -reach), reach).astype(held_as)


def setup_inputs(seed: int = 0) -> dict:
    key_list = jax.random.split(jax.random.key(seed), 7)
    queries = draw_queries(jax.random.fold_in(key_list[6], 71), 0)
    hidden_rows = scatter_about(key_list[1], (SEGMENT, D), 1.0, 6.0, ((0, 128),))
    kv_weight = scatter_about(key_list[2], (2, D, KVD), D ** -0.5, 0.0625, ((2, 4),))
    cache_keys = draw_cache_keys(jax.random.fold_in(key_list[6], 71), 0)
    cache_values = scatter_about(key_list[4], (N_GROUP * PREFIX_CAP, KVD), 1.0, 6.0, ((0, 32), (1, 4)))
    kv_blocks = uneven_parts(key_list[5], N_GROUP, N_GROUP * NBLK // 2, NBLK, 1).astype(jnp.int32)
    return {"queries": queries, "hidden_rows": hidden_rows, "kv_weight": kv_weight, "cache_keys": cache_keys, "cache_values": cache_values, "kv_blocks": kv_blocks}


def rotate(key_proj, positions, head_dim):
    rows = key_proj.shape[0]
    half = head_dim // 2
    heads3 = key_proj.reshape(rows, -1, head_dim)
    freq = jnp.exp(jnp.arange(half, dtype=jnp.float32) * (-2.0 * math.log(500000.0) / head_dim))
    angle = positions.astype(jnp.float32)[:, None] * freq[None, :]
    cosine = jnp.cos(angle)[:, None, :]
    sine = jnp.sin(angle)[:, None, :]
    first = heads3[..., :half]
    second = heads3[..., half:]
    turned = jnp.concatenate([first * cosine - second * sine, second * cosine + first * sine], -1)
    return turned.reshape(rows, -1)

def block_part(scores, visible):
    top_block = lax.optimization_barrier(jnp.max(jnp.where(visible, scores, -1e+30), -1))
    weights = jnp.where(visible, jnp.exp(scores - top_block[..., None]), 0.0)
    rounded = lax.optimization_barrier(weights.astype(jnp.bfloat16)).astype(jnp.float32)
    return (top_block, lax.optimization_barrier(jnp.sum(weights, -1)), rounded)

def reference(queries, hidden_rows, kv_weight, cache_keys, cache_values, kv_blocks):
    key_proj = jnp.dot(hidden_rows, kv_weight[0], preferred_element_type=jnp.float32)
    new_values = jnp.dot(hidden_rows, kv_weight[1], preferred_element_type=jnp.float32).astype(jnp.bfloat16)
    prefix_len = jnp.sum(kv_blocks) * BLOCK
    positions = prefix_len + jnp.arange(SEGMENT, dtype=jnp.int32)
    new_keys = rotate(key_proj, positions, HEAD_DIM).astype(jnp.bfloat16)
    groups = N_GROUP
    share = HEADS // KV_HEADS
    cache_key4 = cache_keys.astype(jnp.float32).reshape(groups, PREFIX_CAP, KV_HEADS, HEAD_DIM)
    cache_val4 = cache_values.astype(jnp.float32).reshape(groups, PREFIX_CAP, KV_HEADS, HEAD_DIM)
    new_key4 = new_keys.astype(jnp.float32).reshape(groups, NEW_ROWS, KV_HEADS, HEAD_DIM)
    new_val4 = new_values.astype(jnp.float32).reshape(groups, NEW_ROWS, KV_HEADS, HEAD_DIM)
    live = jnp.arange(PREFIX_CAP, dtype=jnp.int32)[None, :] < (kv_blocks * BLOCK)[:, None]
    key_rows = jnp.arange(SEGMENT, dtype=jnp.int32).reshape(groups, NEW_ROWS)
    query_blocks = queries.astype(jnp.float32).reshape(groups, NEW_ROWS, KV_HEADS, share, HEAD_DIM)
    scale = 1.0 / math.sqrt(HEAD_DIM)
    highest = lax.Precision.HIGHEST

    def attend_one(position):
        gidx = position // KV_HEADS
        head = position % KV_HEADS
        query = query_blocks[gidx][:, head]
        cache_head = cache_key4[:, :, head]
        cache_vals = cache_val4[:, :, head]
        new_head = new_key4[:, :, head]
        new_vals = new_val4[:, :, head]
        query_rows = gidx * NEW_ROWS + jnp.arange(NEW_ROWS, dtype=jnp.int32)
        cache_seen = live[None, None, :, :]
        new_seen = key_rows[None, None, :, :] <= query_rows[:, None, None, None]
        cache_scores = jnp.einsum('rsd,gpd->rsgp', query, cache_head, precision=highest) * scale
        new_scores = jnp.einsum('rsd,gpd->rsgp', query, new_head, precision=highest) * scale
        top_cache, den_cache, weight_cache = block_part(cache_scores, cache_seen)
        top_new, den_new, weight_new = block_part(new_scores, new_seen)
        highest_top = jnp.maximum(lax.optimization_barrier(jnp.max(top_cache, -1)), lax.optimization_barrier(jnp.max(top_new, -1)))
        factor_cache = jnp.exp(top_cache - highest_top[..., None])
        factor_new = jnp.exp(top_new - highest_top[..., None])
        numerator = jnp.einsum('rsgp,gpd->rsd', weight_cache * factor_cache[..., None], cache_vals, precision=highest)
        numerator = numerator + jnp.einsum('rsgp,gpd->rsd', weight_new * factor_new[..., None], new_vals, precision=highest)
        denominator = lax.optimization_barrier(jnp.sum(den_cache * factor_cache, -1)) + lax.optimization_barrier(jnp.sum(den_new * factor_new, -1))
        return numerator / denominator[..., None]
    results = lax.map(attend_one, jnp.arange(groups * KV_HEADS, dtype=jnp.int32))
    attended = results.reshape(groups, KV_HEADS, NEW_ROWS, share, HEAD_DIM).transpose(0, 2, 1, 3, 4)
    attended = attended.reshape(SEGMENT, QD).astype(jnp.bfloat16)
    return (attended, new_keys, new_values)
```

```python
import functools
import math

import jax
import jax.numpy as jnp
from jax import lax
from jax.experimental import pallas as pl
from jax.experimental.pallas import tpu as pltpu
from jax.sharding import PartitionSpec as P

HEAD_DIM = 128
BLOCK = 32
ROWS = 128
SHARE = 8
SIDE = 4
EXPONENT = math.log2(math.e) / math.sqrt(HEAD_DIM)
BACK = (0, 1, 3, 2)
VMEM = pl.BlockSpec(memory_space=pltpu.VMEM)
SMEM = pl.BlockSpec(memory_space=pltpu.SMEM)
F32 = jnp.float32
BF16 = jnp.bfloat16


def swap_cores():
    return [(i, i ^ 1) for i in range(2 * SIDE * SIDE)]


def along(phase, distance):
    pairs = []
    for y in range(SIDE):
        for z in range(SIDE):
            for core in range(2):
                if (core + phase) % 2 == 0:
                    to = (y, (z + distance) % SIDE)
                else:
                    to = ((y + distance) % SIDE, z)
                pairs.append(((y * SIDE + z) * 2 + core, (to[0] * SIDE + to[1]) * 2 + core))
    return pairs


def ring(distance):
    return [(x, (x + distance) % SIDE) for x in range(SIDE)]


def sender(info, piece, slot):
    core, y, z = info[0], info[1], info[2]
    first, second = BACK[slot], BACK[piece]
    dy = jnp.where(core == 0, second, first)
    dz = jnp.where(core == 0, first, second)
    return lax.rem(y - dy + SIDE, SIDE) * SIDE + lax.rem(z - dz + SIDE, SIDE)


def pack_kernel(info, keys, values, queries, mine, give, own_queries):
    core = info[0]
    width = SHARE * HEAD_DIM
    for which, target, target_queries, start in (
        (core, mine, own_queries, 0),
        (1 - core, give, give, 2 * ROWS),
    ):
        head = pl.ds(pl.multiple_of(which * HEAD_DIM, HEAD_DIM), HEAD_DIM)
        target[0:ROWS, :] = keys[:, head]
        target[ROWS : 2 * ROWS, :] = values[:, head]
        for h in range(SHARE):
            columns = pl.ds(pl.multiple_of(which * width + h * HEAD_DIM, HEAD_DIM), HEAD_DIM)
            target_queries[start + h * ROWS : start + (h + 1) * ROWS, :] = queries[:, columns]


def pack(info, keys, values, queries):
    return pl.pallas_call(
        pack_kernel,
        out_shape=(
            jax.ShapeDtypeStruct((2 * ROWS, HEAD_DIM), BF16),
            jax.ShapeDtypeStruct(((2 + SHARE) * ROWS, HEAD_DIM), BF16),
            jax.ShapeDtypeStruct((SHARE * ROWS, HEAD_DIM), BF16),
        ),
        in_specs=[SMEM, VMEM, VMEM, VMEM],
        out_specs=(VMEM, VMEM, VMEM),
        name="pack",
    )(info, keys, values, queries)


def project_kernel(info, *refs):
    pieces, (weight, cosine, sine) = refs[:7], refs[7:10]
    new_keys, new_values, mine, give, rows = refs[10:]
    core, x = info[0], info[3]
    size = pieces[1].shape[0]
    rows[pl.ds(pl.multiple_of(x * 2 * size, size), 2 * size), :] = pieces[0][...]
    for piece, back, half in zip(pieces[1:], (1, 3, 1, 3, 2, 2), (0, 1, 1, 0, 0, 1)):
        place = lax.rem(x - back + SIDE, SIDE) * 2 + half
        rows[pl.ds(pl.multiple_of(place * size, size), size), :] = piece[...]
    depth = weight.shape[1]
    step = 1024

    def add(i, totals):
        part = pl.ds(pl.multiple_of(i * step, step), step)
        block = rows[:, part]
        return tuple(
            total + jnp.dot(block, weight[k, part, :], preferred_element_type=F32)
            for k, total in enumerate(totals)
        )

    zero = jnp.zeros((ROWS, 2 * HEAD_DIM), F32)
    keys, values = lax.fori_loop(0, depth // step, add, (zero, zero))
    for h in range(2):
        head = slice(h * HEAD_DIM, (h + 1) * HEAD_DIM)
        key = keys[:, head]
        turned = key * cosine[...] + pltpu.roll(key, HEAD_DIM // 2, 1) * sine[...]
        new_keys[:, head] = turned.astype(BF16)
        new_values[:, head] = values[:, head].astype(BF16)
    for which, target in ((core, mine), (1 - core, give)):
        head = pl.ds(pl.multiple_of(which * HEAD_DIM, HEAD_DIM), HEAD_DIM)
        target[0:ROWS, :] = new_keys[:, head]
        target[ROWS : 2 * ROWS, :] = new_values[:, head]


def project(info, pieces, weight, cosine, sine):
    wide = jax.ShapeDtypeStruct((ROWS, 2 * HEAD_DIM), BF16)
    tall = jax.ShapeDtypeStruct((2 * ROWS, HEAD_DIM), BF16)
    return pl.pallas_call(
        project_kernel,
        out_shape=(wide, wide, tall, tall),
        in_specs=[SMEM] + [VMEM] * 10,
        out_specs=(VMEM,) * 4,
        scratch_shapes=[pltpu.VMEM((ROWS, weight.shape[1]), BF16)],
        compiler_params=pltpu.CompilerParams(vmem_limit_bytes=32 << 20),
        name="project",
    )(info, *pieces, weight, cosine, sine)


def absorb(query, turned_keys, values, state, visible=None):
    top, den, num = state
    scores = jnp.dot(query, turned_keys, preferred_element_type=F32)
    if visible is not None:
        scores = jnp.where(visible, scores, -1e30)
    raised = jnp.maximum(top, jnp.max(scores, axis=1, keepdims=True))
    weights = [
        jnp.exp2((scores[:, i : i + HEAD_DIM] - raised) * EXPONENT)
        for i in range(0, scores.shape[1], HEAD_DIM)
    ]
    keep = jnp.exp2((top - raised) * EXPONENT)
    den = den * keep + functools.reduce(lambda a, b: a + b, weights)
    rounded = jnp.concatenate([w.astype(BF16) for w in weights], 1)
    num = num * keep + jnp.dot(rounded, values, preferred_element_type=F32)
    return raised, den, num


def query_of(own_queries, received, head):
    row = pl.multiple_of(head * ROWS, ROWS)
    there = pl.multiple_of(head * ROWS + 2 * ROWS, ROWS)
    return jnp.concatenate([own_queries[pl.ds(row, ROWS), :], received[pl.ds(there, ROWS), :]], 0)


def cache_kernel(live_keys, info, kv_blocks, own_queries, received, *refs):
    pieces, states = refs[:4], refs[4:7]
    keys, values, turned = refs[7:]
    core = info[0]
    place = jnp.int32(0)
    for piece in range(SIDE):
        for slot in range(SIDE):
            chip = sender(info, piece, slot)
            for half in range(2):
                group = chip * 2 + (core if half == 0 else 1 - core)
                row = slot * 4 * ROWS + half * 2 * ROWS
                there = pl.ds(pl.multiple_of(place, BLOCK), ROWS)
                keys[there, :] = pieces[piece][row : row + ROWS, :]
                values[there, :] = pieces[piece][row + ROWS : row + 2 * ROWS, :]
                place = place + kv_blocks[group] * BLOCK
    for i in range(0, live_keys, 256):
        turned[:, i : i + 256] = keys[i : i + 256, :].T
    size = 2 * ROWS
    step = 512

    def one_head(head, _):
        query = query_of(own_queries, received, head)
        state = (
            jnp.full((size, HEAD_DIM), -1e30, F32),
            jnp.zeros((size, HEAD_DIM), F32),
            jnp.zeros((size, HEAD_DIM), F32),
        )
        for i in range(0, live_keys, step):
            state = absorb(query, turned[:, i : i + step], values[i : i + step, :], state)
        rows = pl.ds(pl.multiple_of(head * size, size), size)
        for ref, value in zip(states, state):
            ref[rows, :] = value
        return 0

    lax.fori_loop(0, SHARE, one_head, 0)


STATE = jax.ShapeDtypeStruct((2 * SHARE * ROWS, HEAD_DIM), F32)


def attend_cache(info, kv_blocks, own_queries, received, pieces, live_keys):
    return pl.pallas_call(
        functools.partial(cache_kernel, live_keys),
        out_shape=(STATE,) * 3,
        in_specs=[SMEM, SMEM] + [VMEM] * 6,
        out_specs=(VMEM,) * 3,
        scratch_shapes=[
            pltpu.VMEM((live_keys + ROWS, HEAD_DIM), BF16),
            pltpu.VMEM((live_keys + ROWS, HEAD_DIM), BF16),
            pltpu.VMEM((HEAD_DIM, live_keys), BF16),
        ],
        compiler_params=pltpu.CompilerParams(vmem_limit_bytes=24 << 20),
        name="attend_cache",
    )(info, kv_blocks, own_queries, received, *pieces)


def new_kernel(which, last, info, own_queries, received, *refs):
    count = len(which)
    pieces, states = refs[:count], refs[count : count + 3]
    outs, (turned,) = refs[count + 3 : -1], refs[-1:]
    core, me = info[0], info[1] * SIDE + info[2]
    size = 2 * ROWS
    if not last:
        for ref, old in zip(outs, states):
            ref[...] = old[...]
        states = outs

    def visit(ref, slot, visible):
        base = slot * 4 * ROWS
        keys = jnp.concatenate(
            [ref[base : base + ROWS, :], ref[base + 2 * ROWS : base + 3 * ROWS, :]], 0
        )
        turned[...] = keys.T

        def one_head(head, _):
            rows = pl.ds(pl.multiple_of(head * size, size), size)
            values = jnp.concatenate(
                [
                    ref[base + ROWS : base + 2 * ROWS, :],
                    ref[base + 3 * ROWS : base + 4 * ROWS, :],
                ],
                0,
            )
            state = absorb(
                query_of(own_queries, received, head),
                turned[...],
                values,
                tuple(s[rows, :] for s in states),
                visible() if visible else None,
            )
            for s, value in zip(states, state):
                s[rows, :] = value
            return 0

        lax.fori_loop(0, SHARE, one_head, 0)

    def causal():
        def position(axis):
            at = lax.broadcasted_iota(jnp.int32, (size, size), axis)
            return jnp.where(core == 0, at, lax.rem(at + ROWS, size))

        return position(1) <= position(0)

    for piece, ref in zip(which, pieces):
        for slot in range(SIDE):
            if piece == 0 and slot == 0:
                visit(ref, slot, causal)
                continue
            pl.when(sender(info, piece, slot) < me)(
                functools.partial(visit, ref, slot, None)
            )
    if last:
        here, there = outs

        for head in range(SHARE):
            rows = slice(head * size, (head + 1) * size)
            den = jnp.sum(states[1][rows, :], axis=1, keepdims=True)
            result = (states[2][rows, :] / den).astype(BF16)
            columns = slice(head * HEAD_DIM, (head + 1) * HEAD_DIM)
            here[:, columns] = result[:ROWS]
            there[:, columns] = result[ROWS:]


def attend_new(info, own_queries, received, which, pieces, states, last):
    out = jax.ShapeDtypeStruct((ROWS, SHARE * HEAD_DIM), BF16)
    aliases = {} if last else {3 + len(which) + i: i for i in range(3)}
    return pl.pallas_call(
        functools.partial(new_kernel, which, last),
        out_shape=(out, out) if last else (STATE,) * 3,
        in_specs=[SMEM] + [VMEM] * (2 + len(which) + 3),
        out_specs=(VMEM,) * (2 if last else 3),
        scratch_shapes=[pltpu.VMEM((HEAD_DIM, 2 * ROWS), BF16)],
        compiler_params=pltpu.CompilerParams(vmem_limit_bytes=24 << 20),
        name="attend_new_last" if last else "attend_new",
    )(info, own_queries, received, *pieces, *states)


def spread(block):
    first = [block] + [lax.ppermute(block, "group", along(0, d)) for d in (1, 3, 2)]
    joined = jnp.concatenate(first, 0)
    return [joined] + [lax.ppermute(joined, "group", along(1, d)) for d in (1, 3, 2)]


def shards(queries, hidden_rows, kv_weight, cache_keys, cache_values, kv_blocks):
    group = lax.axis_index("group")
    x = lax.axis_index("tensor")
    core, chip = lax.rem(group, 2), group // 2
    info = jnp.stack([core, chip // SIDE, lax.rem(chip, SIDE), x]).astype(jnp.int32)
    size = hidden_rows.shape[0] // 2
    upper, lower = hidden_rows[:size], hidden_rows[size:]
    upper_right = lax.ppermute(upper, "tensor", ring(1))
    lower_left = lax.ppermute(lower, "tensor", ring(3))
    lower_right = lax.ppermute(lower, "tensor", ring(1))
    upper_left = lax.ppermute(upper, "tensor", ring(3))
    upper_far = lax.ppermute(upper_right, "tensor", ring(1))
    lower_far = lax.ppermute(lower_left, "tensor", ring(3))

    mine, give, own_queries = pack(info, cache_keys, cache_values, queries)
    received = lax.ppermute(give, "group", swap_cores())
    cache = spread(jnp.concatenate([mine, received[: 2 * ROWS]], 0))
    live_keys = cache_keys.shape[0] * kv_blocks.shape[0] // 2
    states = attend_cache(info, kv_blocks, own_queries, received, cache, live_keys)

    half = HEAD_DIM // 2
    positions = jnp.sum(kv_blocks) * BLOCK + group * ROWS + jnp.arange(ROWS, dtype=jnp.int32)
    freq = jnp.exp(jnp.arange(half, dtype=F32) * (-2.0 * math.log(500000.0) / HEAD_DIM))
    angle = positions.astype(F32)[:, None] * freq[None, :]
    cosine, sine = jnp.cos(angle), jnp.sin(angle)
    new_keys, new_values, mine, give = project(
        info,
        (hidden_rows, upper_right, lower_left, lower_right, upper_left, upper_far, lower_far),
        kv_weight,
        jnp.concatenate([cosine, cosine], 1),
        jnp.concatenate([-sine, sine], 1),
    )
    new = spread(jnp.concatenate([mine, lax.ppermute(give, "group", swap_cores())], 0))
    states = attend_new(info, own_queries, received, (0,), new[:1], states, False)
    states = attend_new(info, own_queries, received, (1, 2), new[1:3], states, False)
    here, there = attend_new(info, own_queries, received, (3,), new[3:], states, True)
    other = lax.ppermute(there, "group", swap_cores())
    attended = jnp.where(
        core == 0, jnp.concatenate([here, other], 1), jnp.concatenate([other, here], 1)
    )
    return (attended, new_keys, new_values)


def solution(mesh):
    placed = (
        P("group", "tensor"),
        P(("group", "tensor"), None),
        P(None, None, "tensor"),
        P("group", "tensor"),
        P("group", "tensor"),
        P(),
    )
    return jax.shard_map(
        shards,
        mesh=mesh,
        in_specs=placed,
        out_specs=(P("group", "tensor"), P("group", "tensor"), P("group", "tensor")),
        check_vma=False,
    )
```

```python
import functools
import math

import jax
import jax.numpy as jnp
from jax import lax
from jax.experimental import pallas as pl
from jax.experimental.pallas import tpu as pltpu
from jax.sharding import PartitionSpec as P

HEAD_DIM = 128
BLOCK = 32
ROWS = 128
SHARE = 8
SIDE = 4
EXPONENT = math.log2(math.e) / math.sqrt(HEAD_DIM)
ARRIVAL = (0, 1, 3, 2)
BACK = (0, 1, 3, 2)
VMEM = pl.BlockSpec(memory_space=pltpu.VMEM)
SMEM = pl.BlockSpec(memory_space=pltpu.SMEM)
F32 = jnp.float32
BF16 = jnp.bfloat16


def swap_cores():
    return [(i, i ^ 1) for i in range(2 * SIDE * SIDE)]


def along(phase, distance):
    pairs = []
    for y in range(SIDE):
        for z in range(SIDE):
            for core in range(2):
                if (core + phase) % 2 == 0:
                    to = (y, (z + distance) % SIDE)
                else:
                    to = ((y + distance) % SIDE, z)
                pairs.append(((y * SIDE + z) * 2 + core, (to[0] * SIDE + to[1]) * 2 + core))
    return pairs


def ring(distance):
    pairs = []
    for group in range(2 * SIDE * SIDE):
        for x in range(SIDE):
            to = (x + (distance if group % 2 == 0 else -distance)) % SIDE
            pairs.append((group * SIDE + x, group * SIDE + to))
    return pairs


def place():
    group = lax.axis_index("group")
    return lax.rem(group, 2), group // (2 * SIDE), lax.rem(group // 2, SIDE)


def sender(piece, slot):
    core, y, z = place()
    first, second = BACK[slot], BACK[piece]
    dy = jnp.where(core == 0, second, first)
    dz = jnp.where(core == 0, first, second)
    return lax.rem(y - dy + SIDE, SIDE) * SIDE + lax.rem(z - dz + SIDE, SIDE)


def cost(microseconds):
    return pl.CostEstimate(
        flops=int(microseconds * 1.1e9), bytes_accessed=int(microseconds * 3.5e6), transcendentals=0
    )


def heads_kernel(width, *refs):
    core, _, _ = place()
    arrays, (mine, give) = refs[:-2], refs[-2:]
    for which, target in ((core, mine), (1 - core, give)):
        at = 0
        for array in arrays:
            for i in range(0, width, HEAD_DIM):
                columns = pl.ds(pl.multiple_of(which * width + i, HEAD_DIM), HEAD_DIM)
                target[at : at + ROWS, :] = array[:, columns]
                at += ROWS


def heads(width, *arrays):
    rows = len(arrays) * width // HEAD_DIM * ROWS
    tall = jax.ShapeDtypeStruct((rows, HEAD_DIM), BF16)
    return pl.pallas_call(
        functools.partial(heads_kernel, width),
        out_shape=(tall, tall),
        in_specs=[VMEM] * len(arrays),
        out_specs=(VMEM,) * 2,
        compiler_params=pltpu.CompilerParams(vmem_limit_bytes=8 << 20),
        cost_estimate=cost(0.1),
        name="heads",
    )(*arrays)


def sent_from(step):
    core, _, _ = place()
    x = lax.axis_index("tensor")
    return lax.rem(jnp.where(core == 0, x - step, x + step) + SIDE, SIDE)


def near_kernel(*refs):
    pieces, weight, keys_out, values_out, held, rows, sems = refs[:3], *refs[3:]
    chunks = sems.shape[0]
    step = held.shape[1] // chunks

    def fetch(i):
        part = pl.ds(i * step, step)
        return pltpu.make_async_copy(weight.at[:, part, :], held.at[:, part, :], sems.at[i])

    for i in range(chunks):
        fetch(i).start()
    size = pieces[0].shape[0]
    for i, piece in enumerate(pieces):
        rows[i * size : (i + 1) * size, :] = piece[...]
    keys = jnp.zeros(keys_out.shape, F32)
    values = jnp.zeros(keys_out.shape, F32)
    for i in range(chunks):
        fetch(i).wait()
        part = slice(i * step, (i + 1) * step)
        keys += jnp.dot(rows[:, part], held[0, part, :], preferred_element_type=F32)
        values += jnp.dot(rows[:, part], held[1, part, :], preferred_element_type=F32)
    keys_out[...] = keys
    values_out[...] = values


def project_near(pieces, weight):
    count = sum(piece.shape[0] for piece in pieces)
    wide = jax.ShapeDtypeStruct((count, weight.shape[2]), F32)
    return pl.pallas_call(
        near_kernel,
        out_shape=(wide, wide, jax.ShapeDtypeStruct(weight.shape, BF16)),
        in_specs=[VMEM] * 3 + [pl.BlockSpec(memory_space=pltpu.HBM)],
        out_specs=(VMEM,) * 3,
        scratch_shapes=[
            pltpu.VMEM((count, weight.shape[1]), BF16),
            pltpu.SemaphoreType.DMA((8,)),
        ],
        compiler_params=pltpu.CompilerParams(vmem_limit_bytes=32 << 20),
        cost_estimate=cost(0.1),
        name="project_near",
    )(*pieces, weight)


def far_kernel(piece, near_keys, near_values, weight, cosine, sine, *refs):
    new_keys, new_values, mine, give = refs
    size = piece.shape[0]
    keys = jnp.zeros((size, weight.shape[2]), F32)
    values = jnp.zeros((size, weight.shape[2]), F32)
    step = 1024
    for i in range(0, piece.shape[1], step):
        part = slice(i, i + step)
        keys += jnp.dot(piece[:, part], weight[0, part, :], preferred_element_type=F32)
        values += jnp.dot(piece[:, part], weight[1, part, :], preferred_element_type=F32)
    for i, back in enumerate(ARRIVAL):
        at = pl.ds(pl.multiple_of(sent_from(back) * size, size), size)
        part = slice(i * size, (i + 1) * size)
        last = i == len(ARRIVAL) - 1
        for h in range(2):
            head = slice(h * HEAD_DIM, (h + 1) * HEAD_DIM)
            key = keys[:, head] if last else near_keys[part, head]
            turned = key * cosine[at, :] + pltpu.roll(key, HEAD_DIM // 2, 1) * sine[at, :]
            new_keys[at, head] = turned.astype(BF16)
        value = values if last else near_values[part, :]
        new_values[at, :] = value.astype(BF16)
    core, _, _ = place()
    for which, target in ((core, mine), (1 - core, give)):
        head = pl.ds(pl.multiple_of(which * HEAD_DIM, HEAD_DIM), HEAD_DIM)
        target[0:ROWS, :] = new_keys[:, head]
        target[ROWS : 2 * ROWS, :] = new_values[:, head]


def project_far(piece, near_keys, near_values, weight, cosine, sine):
    wide = jax.ShapeDtypeStruct((ROWS, 2 * HEAD_DIM), BF16)
    tall = jax.ShapeDtypeStruct((2 * ROWS, HEAD_DIM), BF16)
    return pl.pallas_call(
        far_kernel,
        out_shape=(wide, wide, tall, tall),
        in_specs=[VMEM] * 6,
        out_specs=(VMEM,) * 4,
        compiler_params=pltpu.CompilerParams(vmem_limit_bytes=24 << 20),
        cost_estimate=cost(0.1),
        name="project_far",
    )(piece, near_keys, near_values, weight, cosine, sine)


def absorb(query, turned_keys, values, state, visible=None):
    top, den, num = state
    scores = jnp.dot(query, turned_keys, preferred_element_type=F32)
    if visible is not None:
        scores = jnp.where(visible, scores, -1e30)
    raised = jnp.maximum(top, jnp.max(scores, axis=1, keepdims=True))
    weights = [
        jnp.exp2((scores[:, i : i + HEAD_DIM] - raised) * EXPONENT)
        for i in range(0, scores.shape[1], HEAD_DIM)
    ]
    keep = jnp.exp2((top - raised) * EXPONENT)
    den = den * keep + functools.reduce(lambda a, b: a + b, weights)
    rounded = jnp.concatenate([w.astype(BF16) for w in weights], 1)
    num = num * keep + jnp.dot(rounded, values, preferred_element_type=F32)
    return raised, den, num


TILE = 512


def tiles(own_queries, received):
    found = []
    for i in range(0, SHARE * ROWS, TILE):
        found.append((0, i, functools.partial(own_queries.__getitem__, slice(i, i + TILE))))
    for i in range(0, SHARE * ROWS, TILE):
        there = slice(i, i + TILE)
        found.append((1, SHARE * ROWS + i, functools.partial(received.__getitem__, there)))
    return found


STATE = jax.ShapeDtypeStruct((2 * SHARE * ROWS, HEAD_DIM), F32)


def cache_kernel(live_keys, kv_blocks, own_queries, received, *refs):
    pieces, states, (keys, values, turned) = refs[:4], refs[4:7], refs[7:]
    core, _, _ = place()
    at = jnp.int32(0)
    for piece in range(SIDE):
        for slot in range(SIDE):
            chip = sender(piece, slot)
            for half in range(2):
                group = chip * 2 + (core if half == 0 else 1 - core)
                row = slot * 4 * ROWS + half * 2 * ROWS
                there = pl.ds(pl.multiple_of(at, BLOCK), ROWS)
                keys[there, :] = pieces[piece][row : row + ROWS, :]
                values[there, :] = pieces[piece][row + ROWS : row + 2 * ROWS, :]
                at = at + kv_blocks[group] * BLOCK
    for i in range(0, live_keys, 256):
        turned[:, i : i + 256] = keys[i : i + 256, :].T
    for _, start, query in tiles(own_queries, received):
        zero = jnp.zeros((TILE, HEAD_DIM), F32)
        state = (jnp.full((TILE, HEAD_DIM), -1e30, F32), zero, zero)
        state = absorb(query(), turned[...], values[:live_keys, :], state)
        for ref, value in zip(states, state):
            ref[start : start + TILE, :] = value


def attend_cache(kv_blocks, own_queries, received, pieces, live_keys):
    held = pltpu.VMEM((live_keys + ROWS, HEAD_DIM), BF16)
    return pl.pallas_call(
        functools.partial(cache_kernel, live_keys),
        out_shape=(STATE,) * 3,
        in_specs=[SMEM] + [VMEM] * 6,
        out_specs=(VMEM,) * 3,
        scratch_shapes=[held, held, pltpu.VMEM((HEAD_DIM, live_keys), BF16)],
        compiler_params=pltpu.CompilerParams(vmem_limit_bytes=24 << 20),
        cost_estimate=cost(0.1),
        name="attend_cache",
    )(kv_blocks, own_queries, received, *pieces)


def new_kernel(which, last, own_queries, received, *refs):
    count = len(which)
    pieces, olds = refs[:count], refs[count : count + 3]
    outs, (turned, held), sums = refs[count + 3 :], refs[-5:-3], refs[-3:]
    core, y, z = place()
    size = 2 * ROWS
    if not last:
        sums = outs[:3]
    parts = tiles(own_queries, received)

    def visit(keys, values, sources, visible=None):
        for partner, start, query in parts:
            rows = slice(start, start + TILE)
            state = absorb(
                query(),
                keys,
                values,
                tuple(s[rows, :] for s in sources),
                visible(partner) if visible else None,
            )
            for s, value in zip(sums, state):
                s[rows, :] = value

    def block_of(ref, slot):
        base = slot * 4 * ROWS
        here = [slice(base + i * ROWS, base + (i + 1) * ROWS) for i in range(4)]
        keys = jnp.concatenate([ref[here[0], :], ref[here[2], :]], 0)
        return keys.T, jnp.concatenate([ref[here[1], :], ref[here[3], :]], 0)

    def causal(partner):
        shape = (TILE, size)
        row = lax.rem(lax.broadcasted_iota(jnp.int32, shape, 0), ROWS)
        row = row + jnp.where(core == partner, 0, ROWS)
        key = lax.broadcasted_iota(jnp.int32, shape, 1)
        key = jnp.where(core == 0, key, lax.rem(key + ROWS, size))
        return key <= row

    found = jnp.int32(0)
    for piece, ref in zip(which, pieces):
        for slot in range(SIDE):
            if piece == 0 and slot == 0:
                continue
            seen = sender(piece, slot) < y * SIDE + z

            def keep(ref=ref, slot=slot, found=found):
                there = pl.ds(pl.multiple_of(found * size, size), size)
                turned[:, there], held[there, :] = block_of(ref, slot)

            pl.when(seen)(keep)
            found = found + seen.astype(jnp.int32)

    def one(i, sources):
        there = pl.ds(pl.multiple_of(i * size, size), size)
        visit(turned[:, there], held[there, :], sources)

    def rest(first):
        def body(i, _):
            one(i, sums)
            return 0

        lax.fori_loop(first, found, body, 0)

    if which[0] == 0:
        visit(*block_of(pieces[0], 0), olds, causal)
        rest(0)
    else:

        @pl.when(found == 0)
        def _():
            for new, old in zip(sums, olds):
                new[...] = old[...]

        @pl.when(found > 0)
        def _():
            one(0, olds)
            rest(1)

    if last:
        here, there = outs[:2]
        for partner, target in ((0, here), (1, there)):
            for head in range(SHARE):
                start = (partner * SHARE + head) * ROWS
                rows = slice(start, start + ROWS)
                den = jnp.sum(sums[1][rows, :], axis=1, keepdims=True)
                columns = slice(head * HEAD_DIM, (head + 1) * HEAD_DIM)
                target[:, columns] = (sums[2][rows, :] / den).astype(BF16)


def attend_new(own_queries, received, which, pieces, states, last):
    out = jax.ShapeDtypeStruct((ROWS, SHARE * HEAD_DIM), BF16)
    blocks = SIDE * len(which)
    total = pltpu.VMEM(STATE.shape if last else (8, HEAD_DIM), F32)
    return pl.pallas_call(
        functools.partial(new_kernel, which, last),
        out_shape=(out, out) if last else (STATE,) * 3,
        in_specs=[VMEM] * (2 + len(which) + 3),
        out_specs=(VMEM,) * (2 if last else 3),
        scratch_shapes=[
            pltpu.VMEM((HEAD_DIM, 2 * ROWS * blocks), BF16),
            pltpu.VMEM((2 * ROWS * blocks, HEAD_DIM), BF16),
            total,
            total,
            total,
        ],
        compiler_params=pltpu.CompilerParams(vmem_limit_bytes=24 << 20),
        cost_estimate=cost(0.1),
        name="attend_new_last" if last else "attend_new",
    )(own_queries, received, *pieces, *states)


def after(value, *others):
    return lax.optimization_barrier((value, *others))[0]


def first_phase(block):
    return jnp.concatenate(
        [block] + [lax.ppermute(block, "group", along(0, d)) for d in (1, 3, 2)], 0
    )


def second_phase(joined):
    return [joined] + [lax.ppermute(joined, "group", along(1, d)) for d in (1, 3, 2)]


def swapped(block):
    return lax.ppermute(block, "group", swap_cores())


def shards(queries, hidden_rows, kv_weight, cache_keys, cache_values, kv_blocks):
    group = lax.axis_index("group")
    core = lax.rem(group, 2)
    both = ("group", "tensor")
    ahead = lax.ppermute(hidden_rows, both, ring(1))
    mine, give = heads(HEAD_DIM, cache_keys, cache_values)
    behind = lax.ppermute(after(hidden_rows, mine), both, ring(3))
    far = lax.ppermute(ahead, both, ring(1))
    cache = second_phase(first_phase(jnp.concatenate([mine, swapped(give)], 0)))

    live_keys = cache_keys.shape[0] * kv_blocks.shape[0] // 2
    half = HEAD_DIM // 2
    positions = live_keys + group * ROWS + jnp.arange(ROWS, dtype=jnp.int32)
    freq = jnp.exp(jnp.arange(half, dtype=F32) * (-2.0 * math.log(500000.0) / HEAD_DIM))
    angle = positions.astype(F32)[:, None] * freq[None, :]
    cosine, sine = jnp.cos(angle), jnp.sin(angle)
    near_keys, near_values, weight = project_near((hidden_rows, ahead, behind), kv_weight)
    own_queries, give_queries = heads(SHARE * HEAD_DIM, after(queries, near_keys))
    received = swapped(give_queries)
    new_keys, new_values, mine, give = project_far(
        after(far, received),
        near_keys,
        near_values,
        weight,
        jnp.concatenate([cosine, cosine], 1),
        jnp.concatenate([-sine, sine], 1),
    )
    joined = first_phase(jnp.concatenate([mine, swapped(give)], 0))
    new = second_phase(joined)
    states = attend_cache(kv_blocks, after(own_queries, joined), received, cache, live_keys)
    states = attend_new(own_queries, received, (0,), new[:1], states, False)
    states = attend_new(own_queries, received, (1, 2), new[1:3], states, False)
    here, there = attend_new(own_queries, received, (3,), new[3:], states, True)
    other = swapped(there)
    attended = jnp.where(
        core == 0, jnp.concatenate([here, other], 1), jnp.concatenate([other, here], 1)
    )
    return (attended, new_keys, new_values)


def solution(mesh):
    placed = (
        P("group", "tensor"),
        P(("group", "tensor"), None),
        P(None, None, "tensor"),
        P("group", "tensor"),
        P("group", "tensor"),
        P(),
    )
    return jax.shard_map(
        shards,
        mesh=mesh,
        in_specs=placed,
        out_specs=(P("group", "tensor"), P("group", "tensor"), P("group", "tensor")),
        check_vma=False,
    )
```

```python
import functools
import math

import jax
import jax.numpy as jnp
from jax import lax
from jax.experimental import pallas as pl
from jax.experimental.pallas import tpu as pltpu
from jax.sharding import PartitionSpec as P

HEAD_DIM = 128
BLOCK = 32
ROWS = 128
SHARE = 8
SIDE = 4
EXPONENT = math.log2(math.e) / math.sqrt(HEAD_DIM)
ARRIVAL = (0, 1, 3, 2)
BACK = (0, 1, 3, 2)
VMEM = pl.BlockSpec(memory_space=pltpu.VMEM)
SMEM = pl.BlockSpec(memory_space=pltpu.SMEM)
F32 = jnp.float32
BF16 = jnp.bfloat16


def swap_cores():
    return [(i, i ^ 1) for i in range(2 * SIDE * SIDE)]


def along(phase, distance):
    pairs = []
    for y in range(SIDE):
        for z in range(SIDE):
            for core in range(2):
                if (core + phase) % 2 == 0:
                    to = (y, (z + distance) % SIDE)
                else:
                    to = ((y + distance) % SIDE, z)
                pairs.append(((y * SIDE + z) * 2 + core, (to[0] * SIDE + to[1]) * 2 + core))
    return pairs


def ring(distance):
    pairs = []
    for group in range(2 * SIDE * SIDE):
        for x in range(SIDE):
            to = (x + (distance if group % 2 == 0 else -distance)) % SIDE
            pairs.append((group * SIDE + x, group * SIDE + to))
    return pairs


def place():
    group = lax.axis_index("group")
    return lax.rem(group, 2), group // (2 * SIDE), lax.rem(group // 2, SIDE)


def sender(piece, slot):
    core, y, z = place()
    first, second = BACK[slot], BACK[piece]
    dy = jnp.where(core == 0, second, first)
    dz = jnp.where(core == 0, first, second)
    return lax.rem(y - dy + SIDE, SIDE) * SIDE + lax.rem(z - dz + SIDE, SIDE)


def cost(microseconds):
    return pl.CostEstimate(
        flops=int(microseconds * 1.1e9), bytes_accessed=int(microseconds * 3.5e6), transcendentals=0
    )


def heads_kernel(width, *refs):
    core, _, _ = place()
    arrays, (mine, give) = refs[:-2], refs[-2:]
    for which, target in ((core, mine), (1 - core, give)):
        at = 0
        for array in arrays:
            for i in range(0, width, HEAD_DIM):
                columns = pl.ds(pl.multiple_of(which * width + i, HEAD_DIM), HEAD_DIM)
                target[at : at + ROWS, :] = array[:, columns]
                at += ROWS


def heads(width, microseconds, *arrays):
    rows = len(arrays) * width // HEAD_DIM * ROWS
    tall = jax.ShapeDtypeStruct((rows, HEAD_DIM), BF16)
    return pl.pallas_call(
        functools.partial(heads_kernel, width),
        out_shape=(tall, tall),
        in_specs=[VMEM] * len(arrays),
        out_specs=(VMEM,) * 2,
        compiler_params=pltpu.CompilerParams(vmem_limit_bytes=4 << 20),
        cost_estimate=cost(microseconds),
        name="heads",
    )(*arrays)


def sent_from(step):
    core, _, _ = place()
    x = lax.axis_index("tensor")
    return lax.rem(jnp.where(core == 0, x - step, x + step) + SIDE, SIDE)


def near_kernel(*refs):
    pieces, weight, keys_out, values_out, rows = refs[:3], *refs[3:]
    size = pieces[0].shape[0]
    for i, piece in enumerate(pieces):
        rows[i * size : (i + 1) * size, :] = piece[...]
    keys = jnp.zeros(keys_out.shape, F32)
    values = jnp.zeros(keys_out.shape, F32)
    step = 1024
    for i in range(0, rows.shape[1], step):
        part = slice(i, i + step)
        keys += jnp.dot(rows[:, part], weight[0, part, :], preferred_element_type=F32)
        values += jnp.dot(rows[:, part], weight[1, part, :], preferred_element_type=F32)
    keys_out[...] = keys
    values_out[...] = values


def project_near(pieces, weight):
    count = sum(piece.shape[0] for piece in pieces)
    wide = jax.ShapeDtypeStruct((count, weight.shape[2]), F32)
    return pl.pallas_call(
        near_kernel,
        out_shape=(wide, wide),
        in_specs=[VMEM] * 4,
        out_specs=(VMEM,) * 2,
        scratch_shapes=[pltpu.VMEM((count, weight.shape[1]), BF16)],
        compiler_params=pltpu.CompilerParams(vmem_limit_bytes=24 << 20),
        cost_estimate=cost(20),
        name="project_near",
    )(*pieces, weight)


def far_kernel(piece, near_keys, near_values, weight, cosine, sine, *refs):
    new_keys, new_values, mine, give = refs
    size = piece.shape[0]
    keys = jnp.zeros((size, weight.shape[2]), F32)
    values = jnp.zeros((size, weight.shape[2]), F32)
    step = 1024
    for i in range(0, piece.shape[1], step):
        part = slice(i, i + step)
        keys += jnp.dot(piece[:, part], weight[0, part, :], preferred_element_type=F32)
        values += jnp.dot(piece[:, part], weight[1, part, :], preferred_element_type=F32)
    for i, back in enumerate(ARRIVAL):
        at = pl.ds(pl.multiple_of(sent_from(back) * size, size), size)
        part = slice(i * size, (i + 1) * size)
        last = i == len(ARRIVAL) - 1
        for h in range(2):
            head = slice(h * HEAD_DIM, (h + 1) * HEAD_DIM)
            key = keys[:, head] if last else near_keys[part, head]
            turned = key * cosine[at, :] + pltpu.roll(key, HEAD_DIM // 2, 1) * sine[at, :]
            new_keys[at, head] = turned.astype(BF16)
        value = values if last else near_values[part, :]
        new_values[at, :] = value.astype(BF16)
    core, _, _ = place()
    for which, target in ((core, mine), (1 - core, give)):
        head = pl.ds(pl.multiple_of(which * HEAD_DIM, HEAD_DIM), HEAD_DIM)
        target[0:ROWS, :] = new_keys[:, head]
        target[ROWS : 2 * ROWS, :] = new_values[:, head]


def project_far(piece, near_keys, near_values, weight, cosine, sine):
    wide = jax.ShapeDtypeStruct((ROWS, 2 * HEAD_DIM), BF16)
    tall = jax.ShapeDtypeStruct((2 * ROWS, HEAD_DIM), BF16)
    return pl.pallas_call(
        far_kernel,
        out_shape=(wide, wide, tall, tall),
        in_specs=[VMEM] * 6,
        out_specs=(VMEM,) * 4,
        compiler_params=pltpu.CompilerParams(vmem_limit_bytes=24 << 20),
        cost_estimate=cost(0.1),
        name="project_far",
    )(piece, near_keys, near_values, weight, cosine, sine)


def absorb(query, turned_keys, values, state, visible=None):
    top, den, num = state
    scores = jnp.dot(query, turned_keys, preferred_element_type=F32)
    if visible is not None:
        scores = jnp.where(visible, scores, -1e30)
    raised = jnp.maximum(top, jnp.max(scores, axis=1, keepdims=True))
    weights = [
        jnp.exp2((scores[:, i : i + HEAD_DIM] - raised) * EXPONENT)
        for i in range(0, scores.shape[1], HEAD_DIM)
    ]
    keep = jnp.exp2((top - raised) * EXPONENT)
    den = den * keep + functools.reduce(lambda a, b: a + b, weights)
    rounded = jnp.concatenate([w.astype(BF16) for w in weights], 1)
    num = num * keep + jnp.dot(rounded, values, preferred_element_type=F32)
    return raised, den, num


TILE = 1024


def tiles(own_queries, received):
    found = []
    for i in range(0, SHARE * ROWS, TILE):
        found.append((0, i, functools.partial(own_queries.__getitem__, slice(i, i + TILE))))
    for i in range(0, SHARE * ROWS, TILE):
        there = slice(i, i + TILE)
        found.append((1, SHARE * ROWS + i, functools.partial(received.__getitem__, there)))
    return found


STATE = jax.ShapeDtypeStruct((2 * SHARE * ROWS, HEAD_DIM), F32)


def cache_kernel(live_keys, kv_blocks, own_queries, received, *refs):
    pieces, states, (keys, values, turned) = refs[:4], refs[4:7], refs[7:]
    core, _, _ = place()
    at = jnp.int32(0)
    for piece in range(SIDE):
        for slot in range(SIDE):
            chip = sender(piece, slot)
            for half in range(2):
                group = chip * 2 + (core if half == 0 else 1 - core)
                row = slot * 4 * ROWS + half * 2 * ROWS
                there = pl.ds(pl.multiple_of(at, BLOCK), ROWS)
                keys[there, :] = pieces[piece][row : row + ROWS, :]
                values[there, :] = pieces[piece][row + ROWS : row + 2 * ROWS, :]
                at = at + kv_blocks[group] * BLOCK
    for i in range(0, live_keys, 256):
        turned[:, i : i + 256] = keys[i : i + 256, :].T
    for _, start, query in tiles(own_queries, received):
        zero = jnp.zeros((TILE, HEAD_DIM), F32)
        state = (jnp.full((TILE, HEAD_DIM), -1e30, F32), zero, zero)
        state = absorb(query(), turned[...], values[:live_keys, :], state)
        for ref, value in zip(states, state):
            ref[start : start + TILE, :] = value


def attend_cache(kv_blocks, own_queries, received, pieces, live_keys):
    held = pltpu.VMEM((live_keys + ROWS, HEAD_DIM), BF16)
    return pl.pallas_call(
        functools.partial(cache_kernel, live_keys),
        out_shape=(STATE,) * 3,
        in_specs=[SMEM] + [VMEM] * 6,
        out_specs=(VMEM,) * 3,
        scratch_shapes=[held, held, pltpu.VMEM((HEAD_DIM, live_keys), BF16)],
        compiler_params=pltpu.CompilerParams(vmem_limit_bytes=24 << 20),
        cost_estimate=cost(0.1),
        name="attend_cache",
    )(kv_blocks, own_queries, received, *pieces)


def new_kernel(which, last, own_queries, received, *refs):
    count = len(which)
    pieces, olds = refs[:count], refs[count : count + 3]
    outs, (turned, held), sums = refs[count + 3 :], refs[-5:-3], refs[-3:]
    core, y, z = place()
    size = 2 * ROWS
    if not last:
        sums = outs[:3]
    parts = tiles(own_queries, received)

    def visit(keys, values, sources, visible=None):
        for partner, start, query in parts:
            rows = slice(start, start + TILE)
            state = absorb(
                query(),
                keys,
                values,
                tuple(s[rows, :] for s in sources),
                visible(partner) if visible else None,
            )
            for s, value in zip(sums, state):
                s[rows, :] = value

    def block_of(ref, slot):
        base = slot * 4 * ROWS
        here = [slice(base + i * ROWS, base + (i + 1) * ROWS) for i in range(4)]
        keys = jnp.concatenate([ref[here[0], :], ref[here[2], :]], 0)
        return keys.T, jnp.concatenate([ref[here[1], :], ref[here[3], :]], 0)

    def causal(partner):
        shape = (TILE, size)
        row = lax.rem(lax.broadcasted_iota(jnp.int32, shape, 0), ROWS)
        row = row + jnp.where(core == partner, 0, ROWS)
        key = lax.broadcasted_iota(jnp.int32, shape, 1)
        key = jnp.where(core == 0, key, lax.rem(key + ROWS, size))
        return key <= row

    found = jnp.int32(0)
    for piece, ref in zip(which, pieces):
        for slot in range(SIDE):
            if piece == 0 and slot == 0:
                continue
            seen = sender(piece, slot) < y * SIDE + z

            def keep(ref=ref, slot=slot, found=found):
                there = pl.ds(pl.multiple_of(found * size, size), size)
                turned[:, there], held[there, :] = block_of(ref, slot)

            pl.when(seen)(keep)
            found = found + seen.astype(jnp.int32)

    def chunk(first, blocks, sources):
        there = pl.ds(pl.multiple_of(first * size, size), blocks * size)
        visit(turned[:, there], held[there, :], sources)

    def rest(first, sources):
        left = found - first

        def body(i, _):
            chunk(first + 4 * i, 4, sources)
            return 0

        lax.fori_loop(0, left // 4, body, 0)
        pl.when((left & 2) != 0)(lambda: chunk(first + (left // 4) * 4, 2, sources))
        pl.when((left & 1) != 0)(lambda: chunk(found - 1, 1, sources))

    if which[0] == 0:
        visit(*block_of(pieces[0], 0), olds, causal)
    else:
        for new, old in zip(sums, olds):
            new[...] = old[...]
    rest(jnp.int32(0), sums)

    if last:
        here, there = outs[:2]
        for partner, target in ((0, here), (1, there)):
            for head in range(SHARE):
                start = (partner * SHARE + head) * ROWS
                rows = slice(start, start + ROWS)
                den = jnp.sum(sums[1][rows, :], axis=1, keepdims=True)
                columns = slice(head * HEAD_DIM, (head + 1) * HEAD_DIM)
                target[:, columns] = (sums[2][rows, :] / den).astype(BF16)


def attend_new(own_queries, received, which, pieces, states, last):
    out = jax.ShapeDtypeStruct((ROWS, SHARE * HEAD_DIM), BF16)
    blocks = SIDE * len(which)
    total = pltpu.VMEM(STATE.shape if last else (8, HEAD_DIM), F32)
    return pl.pallas_call(
        functools.partial(new_kernel, which, last),
        out_shape=(out, out) if last else (STATE,) * 3,
        in_specs=[VMEM] * (2 + len(which) + 3),
        out_specs=(VMEM,) * (2 if last else 3),
        scratch_shapes=[
            pltpu.VMEM((HEAD_DIM, 2 * ROWS * blocks), BF16),
            pltpu.VMEM((2 * ROWS * blocks, HEAD_DIM), BF16),
            total,
            total,
            total,
        ],
        compiler_params=pltpu.CompilerParams(vmem_limit_bytes=24 << 20),
        cost_estimate=cost(0.1),
        name="attend_new_last" if last else "attend_new",
    )(own_queries, received, *pieces, *states)


def after(value, *others):
    return lax.optimization_barrier((value, *others))[0]


def first_phase(block, *others):
    sent = [lax.ppermute(block, "group", along(0, d)) for d in (1, 3, 2)]
    return jnp.concatenate([after(block, *others) if others else block] + sent, 0)


def second_phase(joined):
    return [joined] + [lax.ppermute(joined, "group", along(1, d)) for d in (1, 3)]


def last_phase(joined, *others):
    return lax.ppermute(after(joined, *others), "group", along(1, 2))


def swapped(block):
    return lax.ppermute(block, "group", swap_cores())


def shards(queries, hidden_rows, kv_weight, cache_keys, cache_values, kv_blocks):
    group = lax.axis_index("group")
    core = lax.rem(group, 2)
    both = ("group", "tensor")
    ahead = lax.ppermute(hidden_rows, both, ring(1))
    mine, give = heads(HEAD_DIM, 0.1, cache_keys, cache_values)
    behind = lax.ppermute(after(hidden_rows, mine), both, ring(3))
    block = jnp.concatenate([mine, swapped(give)], 0)
    joined = first_phase(block)
    own_queries, give_queries = heads(SHARE * HEAD_DIM, 20, after(queries, block))
    received = swapped(give_queries)
    far = lax.ppermute(after(ahead, own_queries), both, ring(1))
    cache = second_phase(joined)

    live_keys = cache_keys.shape[0] * kv_blocks.shape[0] // 2
    half = HEAD_DIM // 2
    positions = live_keys + group * ROWS + jnp.arange(ROWS, dtype=jnp.int32)
    freq = jnp.exp(jnp.arange(half, dtype=F32) * (-2.0 * math.log(500000.0) / HEAD_DIM))
    angle = positions.astype(F32)[:, None] * freq[None, :]
    cosine, sine = jnp.cos(angle), jnp.sin(angle)
    near_keys, near_values = project_near((hidden_rows, ahead, behind), kv_weight)
    cache.append(last_phase(joined, near_keys))
    new_keys, new_values, mine, give = project_far(
        after(far, received),
        near_keys,
        near_values,
        kv_weight,
        jnp.concatenate([cosine, cosine], 1),
        jnp.concatenate([-sine, sine], 1),
    )
    block = after(jnp.concatenate([mine, swapped(give)], 0), *cache[:3])
    states = attend_cache(kv_blocks, after(own_queries, block), received, cache, live_keys)
    joined = first_phase(block, states[0])
    new = second_phase(joined)
    states = attend_new(own_queries, received, (0,), new[:1], states, False)
    new.append(last_phase(joined, states[0]))
    states = attend_new(own_queries, received, (1, 2), new[1:3], states, False)
    here, there = attend_new(own_queries, received, (3,), new[3:], states, True)
    other = swapped(there)
    attended = jnp.where(
        core == 0, jnp.concatenate([here, other], 1), jnp.concatenate([other, here], 1)
    )
    return (attended, new_keys, new_values)


def solution(mesh):
    placed = (
        P("group", "tensor"),
        P(("group", "tensor"), None),
        P(None, None, "tensor"),
        P("group", "tensor"),
        P("group", "tensor"),
        P(),
    )
    return jax.shard_map(
        shards,
        mesh=mesh,
        in_specs=placed,
        out_specs=(P("group", "tensor"), P("group", "tensor"), P("group", "tensor")),
        check_vma=False,
    )
```

```python
import functools
import math

import jax
import jax.numpy as jnp
from jax import lax
from jax.experimental import pallas as pl
from jax.experimental.pallas import tpu as pltpu
from jax.sharding import PartitionSpec as P

HEAD_DIM = 128
BLOCK = 32
ROWS = 128
SHARE = 8
SIDE = 4
EXPONENT = math.log2(math.e) / math.sqrt(HEAD_DIM)
ARRIVAL = (0, 1, 3, 2)
BACK = (0, 1, 3, 2)
VMEM = pl.BlockSpec(memory_space=pltpu.VMEM)
SMEM = pl.BlockSpec(memory_space=pltpu.SMEM)
F32 = jnp.float32
BF16 = jnp.bfloat16


def swap_cores():
    return [(i, i ^ 1) for i in range(2 * SIDE * SIDE)]


def along(phase, distance):
    pairs = []
    for y in range(SIDE):
        for z in range(SIDE):
            for core in range(2):
                if (core + phase) % 2 == 0:
                    to = (y, (z + distance) % SIDE)
                else:
                    to = ((y + distance) % SIDE, z)
                pairs.append(((y * SIDE + z) * 2 + core, (to[0] * SIDE + to[1]) * 2 + core))
    return pairs


def ring(distance):
    pairs = []
    for group in range(2 * SIDE * SIDE):
        for x in range(SIDE):
            to = (x + (distance if group % 2 == 0 else -distance)) % SIDE
            pairs.append((group * SIDE + x, group * SIDE + to))
    return pairs


def place():
    group = lax.axis_index("group")
    return lax.rem(group, 2), group // (2 * SIDE), lax.rem(group // 2, SIDE)


def sender(piece, slot):
    core, y, z = place()
    first, second = BACK[slot], BACK[piece]
    dy = jnp.where(core == 0, second, first)
    dz = jnp.where(core == 0, first, second)
    return lax.rem(y - dy + SIDE, SIDE) * SIDE + lax.rem(z - dz + SIDE, SIDE)


def cost(microseconds):
    return pl.CostEstimate(
        flops=int(microseconds * 1.1e9), bytes_accessed=int(microseconds * 3.5e6), transcendentals=0
    )


def heads_kernel(width, *refs):
    core, _, _ = place()
    arrays, (mine, give) = refs[:-2], refs[-2:]
    for which, target in ((core, mine), (1 - core, give)):
        at = 0
        for array in arrays:
            for i in range(0, width, HEAD_DIM):
                columns = pl.ds(pl.multiple_of(which * width + i, HEAD_DIM), HEAD_DIM)
                target[at : at + ROWS, :] = array[:, columns]
                at += ROWS


def heads(width, microseconds, *arrays):
    rows = len(arrays) * width // HEAD_DIM * ROWS
    tall = jax.ShapeDtypeStruct((rows, HEAD_DIM), BF16)
    return pl.pallas_call(
        functools.partial(heads_kernel, width),
        out_shape=(tall, tall),
        in_specs=[VMEM] * len(arrays),
        out_specs=(VMEM,) * 2,
        compiler_params=pltpu.CompilerParams(vmem_limit_bytes=4 << 20),
        cost_estimate=cost(microseconds),
        name="heads",
    )(*arrays)


def sent_from(step):
    core, _, _ = place()
    x = lax.axis_index("tensor")
    return lax.rem(jnp.where(core == 0, x - step, x + step) + SIDE, SIDE)


def near_kernel(*refs):
    pieces, weight, keys_out, values_out, rows = refs[:3], *refs[3:]
    size = pieces[0].shape[0]
    for i, piece in enumerate(pieces):
        rows[i * size : (i + 1) * size, :] = piece[...]
    keys = jnp.zeros(keys_out.shape, F32)
    values = jnp.zeros(keys_out.shape, F32)
    step = 1024
    for i in range(0, rows.shape[1], step):
        part = slice(i, i + step)
        keys += jnp.dot(rows[:, part], weight[0, part, :], preferred_element_type=F32)
        values += jnp.dot(rows[:, part], weight[1, part, :], preferred_element_type=F32)
    keys_out[...] = keys
    values_out[...] = values


def project_near(pieces, weight):
    count = sum(piece.shape[0] for piece in pieces)
    wide = jax.ShapeDtypeStruct((count, weight.shape[2]), F32)
    return pl.pallas_call(
        near_kernel,
        out_shape=(wide, wide),
        in_specs=[VMEM] * 4,
        out_specs=(VMEM,) * 2,
        scratch_shapes=[pltpu.VMEM((count, weight.shape[1]), BF16)],
        compiler_params=pltpu.CompilerParams(vmem_limit_bytes=24 << 20),
        cost_estimate=cost(20),
        name="project_near",
    )(*pieces, weight)


def far_kernel(piece, near_keys, near_values, weight, cosine, sine, *refs):
    new_keys, new_values, mine, give = refs
    size = piece.shape[0]
    keys = jnp.zeros((size, weight.shape[2]), F32)
    values = jnp.zeros((size, weight.shape[2]), F32)
    step = 1024
    for i in range(0, piece.shape[1], step):
        part = slice(i, i + step)
        keys += jnp.dot(piece[:, part], weight[0, part, :], preferred_element_type=F32)
        values += jnp.dot(piece[:, part], weight[1, part, :], preferred_element_type=F32)
    for i, back in enumerate(ARRIVAL):
        at = pl.ds(pl.multiple_of(sent_from(back) * size, size), size)
        part = slice(i * size, (i + 1) * size)
        last = i == len(ARRIVAL) - 1
        for h in range(2):
            head = slice(h * HEAD_DIM, (h + 1) * HEAD_DIM)
            key = keys[:, head] if last else near_keys[part, head]
            turned = key * cosine[at, :] + pltpu.roll(key, HEAD_DIM // 2, 1) * sine[at, :]
            new_keys[at, head] = turned.astype(BF16)
        value = values if last else near_values[part, :]
        new_values[at, :] = value.astype(BF16)
    core, _, _ = place()
    for which, target in ((core, mine), (1 - core, give)):
        head = pl.ds(pl.multiple_of(which * HEAD_DIM, HEAD_DIM), HEAD_DIM)
        target[0:ROWS, :] = new_keys[:, head]
        target[ROWS : 2 * ROWS, :] = new_values[:, head]


def project_far(piece, near_keys, near_values, weight, cosine, sine):
    wide = jax.ShapeDtypeStruct((ROWS, 2 * HEAD_DIM), BF16)
    tall = jax.ShapeDtypeStruct((2 * ROWS, HEAD_DIM), BF16)
    return pl.pallas_call(
        far_kernel,
        out_shape=(wide, wide, tall, tall),
        in_specs=[VMEM] * 6,
        out_specs=(VMEM,) * 4,
        compiler_params=pltpu.CompilerParams(vmem_limit_bytes=24 << 20),
        cost_estimate=cost(0.1),
        name="project_far",
    )(piece, near_keys, near_values, weight, cosine, sine)


def absorb(query, turned_keys, values, state, visible=None):
    top, den, num = state
    scores = jnp.dot(query, turned_keys, preferred_element_type=F32)
    if visible is not None:
        scores = jnp.where(visible, scores, -1e30)
    raised = jnp.maximum(top, jnp.max(scores, axis=1, keepdims=True))
    weights = [
        jnp.exp2((scores[:, i : i + HEAD_DIM] - raised) * EXPONENT)
        for i in range(0, scores.shape[1], HEAD_DIM)
    ]
    keep = jnp.exp2((top - raised) * EXPONENT)
    den = den * keep + functools.reduce(lambda a, b: a + b, weights)
    rounded = jnp.concatenate([w.astype(BF16) for w in weights], 1)
    num = num * keep + jnp.dot(rounded, values, preferred_element_type=F32)
    return raised, den, num


TILE = 1024


def tiles(own_queries, received):
    found = []
    for i in range(0, SHARE * ROWS, TILE):
        found.append((0, i, functools.partial(own_queries.__getitem__, slice(i, i + TILE))))
    for i in range(0, SHARE * ROWS, TILE):
        there = slice(i, i + TILE)
        found.append((1, SHARE * ROWS + i, functools.partial(received.__getitem__, there)))
    return found


STATE = jax.ShapeDtypeStruct((2 * SHARE * ROWS, HEAD_DIM), F32)


def cache_kernel(live_keys, kv_blocks, own_queries, received, *refs):
    pieces, states, (keys, values, turned) = refs[:4], refs[4:7], refs[7:]
    core, _, _ = place()
    at = jnp.int32(0)
    for piece in range(SIDE):
        for slot in range(SIDE):
            chip = sender(piece, slot)
            for half in range(2):
                group = chip * 2 + (core if half == 0 else 1 - core)
                row = slot * 4 * ROWS + half * 2 * ROWS
                there = pl.ds(pl.multiple_of(at, BLOCK), ROWS)
                keys[there, :] = pieces[piece][row : row + ROWS, :]
                values[there, :] = pieces[piece][row + ROWS : row + 2 * ROWS, :]
                at = at + kv_blocks[group] * BLOCK
    for i in range(0, live_keys, 256):
        turned[:, i : i + 256] = keys[i : i + 256, :].T
    for _, start, query in tiles(own_queries, received):
        zero = jnp.zeros((TILE, HEAD_DIM), F32)
        state = (jnp.full((TILE, HEAD_DIM), -1e30, F32), zero, zero)
        state = absorb(query(), turned[...], values[:live_keys, :], state)
        for ref, value in zip(states, state):
            ref[start : start + TILE, :] = value


def attend_cache(kv_blocks, own_queries, received, pieces, live_keys):
    held = pltpu.VMEM((live_keys + ROWS, HEAD_DIM), BF16)
    return pl.pallas_call(
        functools.partial(cache_kernel, live_keys),
        out_shape=(STATE,) * 3,
        in_specs=[SMEM] + [VMEM] * 6,
        out_specs=(VMEM,) * 3,
        scratch_shapes=[held, held, pltpu.VMEM((HEAD_DIM, live_keys), BF16)],
        compiler_params=pltpu.CompilerParams(vmem_limit_bytes=24 << 20),
        cost_estimate=cost(0.1),
        name="attend_cache",
    )(kv_blocks, own_queries, received, *pieces)


def new_kernel(which, last, own_queries, received, *refs):
    count = len(which)
    pieces, olds = refs[:count], refs[count : count + 3]
    outs, (turned, held), sums = refs[count + 3 :], refs[-5:-3], refs[-3:]
    core, y, z = place()
    size = 2 * ROWS
    if not last:
        sums = outs[:3]
    parts = tiles(own_queries, received)

    def visit(keys, values, sources, visible=None):
        for partner, start, query in parts:
            rows = slice(start, start + TILE)
            state = absorb(
                query(),
                keys,
                values,
                tuple(s[rows, :] for s in sources),
                visible(partner) if visible else None,
            )
            for s, value in zip(sums, state):
                s[rows, :] = value

    def block_of(ref, slot):
        base = slot * 4 * ROWS
        here = [slice(base + i * ROWS, base + (i + 1) * ROWS) for i in range(4)]
        keys = jnp.concatenate([ref[here[0], :], ref[here[2], :]], 0)
        return keys.T, jnp.concatenate([ref[here[1], :], ref[here[3], :]], 0)

    def causal(partner):
        shape = (TILE, size)
        row = lax.rem(lax.broadcasted_iota(jnp.int32, shape, 0), ROWS)
        row = row + jnp.where(core == partner, 0, ROWS)
        key = lax.broadcasted_iota(jnp.int32, shape, 1)
        key = jnp.where(core == 0, key, lax.rem(key + ROWS, size))
        return key <= row

    found = jnp.int32(0)
    for piece, ref in zip(which, pieces):
        for slot in range(SIDE):
            if piece == 0 and slot == 0:
                continue
            seen = sender(piece, slot) < y * SIDE + z

            def keep(ref=ref, slot=slot, found=found):
                there = pl.ds(pl.multiple_of(found * size, size), size)
                turned[:, there], held[there, :] = block_of(ref, slot)

            pl.when(seen)(keep)
            found = found + seen.astype(jnp.int32)

    def chunk(first, blocks, sources):
        there = pl.ds(pl.multiple_of(first * size, size), blocks * size)
        visit(turned[:, there], held[there, :], sources)

    def rest(first, sources):
        left = found - first

        def body(i, _):
            chunk(first + 4 * i, 4, sources)
            return 0

        lax.fori_loop(0, left // 4, body, 0)
        pl.when((left & 2) != 0)(lambda: chunk(first + (left // 4) * 4, 2, sources))
        pl.when((left & 1) != 0)(lambda: chunk(found - 1, 1, sources))

    if which[0] == 0:
        visit(*block_of(pieces[0], 0), olds, causal)
    else:
        for new, old in zip(sums, olds):
            new[...] = old[...]
    rest(jnp.int32(0), sums)

    if last:
        here, there = outs[:2]
        for partner, target in ((0, here), (1, there)):
            for head in range(SHARE):
                start = (partner * SHARE + head) * ROWS
                rows = slice(start, start + ROWS)
                den = jnp.sum(sums[1][rows, :], axis=1, keepdims=True)
                columns = slice(head * HEAD_DIM, (head + 1) * HEAD_DIM)
                target[:, columns] = (sums[2][rows, :] / den).astype(BF16)


def attend_new(own_queries, received, which, pieces, states, last):
    out = jax.ShapeDtypeStruct((ROWS, SHARE * HEAD_DIM), BF16)
    blocks = SIDE * len(which)
    total = pltpu.VMEM(STATE.shape if last else (8, HEAD_DIM), F32)
    return pl.pallas_call(
        functools.partial(new_kernel, which, last),
        out_shape=(out, out) if last else (STATE,) * 3,
        in_specs=[VMEM] * (2 + len(which) + 3),
        out_specs=(VMEM,) * (2 if last else 3),
        scratch_shapes=[
            pltpu.VMEM((HEAD_DIM, 2 * ROWS * blocks), BF16),
            pltpu.VMEM((2 * ROWS * blocks, HEAD_DIM), BF16),
            total,
            total,
            total,
        ],
        compiler_params=pltpu.CompilerParams(vmem_limit_bytes=24 << 20),
        cost_estimate=cost(0.1),
        name="attend_new_last" if last else "attend_new",
    )(own_queries, received, *pieces, *states)


def after(value, *others):
    return lax.optimization_barrier((value, *others))[0]


def first_phase(block, *others):
    sent = [lax.ppermute(block, "group", along(0, d)) for d in (1, 3, 2)]
    return jnp.concatenate([after(block, *others) if others else block] + sent, 0)


def second_phase(joined):
    return [joined] + [lax.ppermute(joined, "group", along(1, d)) for d in (1, 3)]


def last_phase(joined, *others):
    return lax.ppermute(after(joined, *others), "group", along(1, 2))


def swapped(block):
    return lax.ppermute(block, "group", swap_cores())


def shards(queries, hidden_rows, kv_weight, cache_keys, cache_values, kv_blocks):
    group = lax.axis_index("group")
    core = lax.rem(group, 2)
    both = ("group", "tensor")
    ahead = lax.ppermute(hidden_rows, both, ring(1))
    mine, give = heads(HEAD_DIM, 0.1, cache_keys, cache_values)
    block = jnp.concatenate([mine, swapped(give)], 0)
    behind = lax.ppermute(after(hidden_rows, block), both, ring(3))
    joined = first_phase(block)
    own_queries, give_queries = heads(SHARE * HEAD_DIM, 5, after(queries, block))
    received = swapped(give_queries)
    far = lax.ppermute(after(ahead, own_queries), both, ring(1))
    cache = second_phase(joined)

    live_keys = cache_keys.shape[0] * kv_blocks.shape[0] // 2
    half = HEAD_DIM // 2
    positions = live_keys + group * ROWS + jnp.arange(ROWS, dtype=jnp.int32)
    freq = jnp.exp(jnp.arange(half, dtype=F32) * (-2.0 * math.log(500000.0) / HEAD_DIM))
    angle = positions.astype(F32)[:, None] * freq[None, :]
    cosine, sine = jnp.cos(angle), jnp.sin(angle)
    near_keys, near_values = project_near((hidden_rows, ahead, behind), kv_weight)
    cache.append(last_phase(joined, near_keys))
    new_keys, new_values, mine, give = project_far(
        after(far, received),
        near_keys,
        near_values,
        kv_weight,
        jnp.concatenate([cosine, cosine], 1),
        jnp.concatenate([-sine, sine], 1),
    )
    block = after(jnp.concatenate([mine, swapped(give)], 0), *cache[:3])
    states = attend_cache(kv_blocks, after(own_queries, block), received, cache, live_keys)
    joined = first_phase(block, states[0])
    new = second_phase(joined)
    states = attend_new(own_queries, received, (0,), new[:1], states, False)
    new.append(last_phase(joined, states[0], new[1]))
    states = attend_new(own_queries, received, (1, 2), new[1:3], states, False)
    here, there = attend_new(own_queries, received, (3,), new[3:], states, True)
    other = swapped(there)
    attended = jnp.where(
        core == 0, jnp.concatenate([here, other], 1), jnp.concatenate([other, here], 1)
    )
    return (attended, new_keys, new_values)


def solution(mesh):
    placed = (
        P("group", "tensor"),
        P(("group", "tensor"), None),
        P(None, None, "tensor"),
        P("group", "tensor"),
        P("group", "tensor"),
        P(),
    )
    return jax.shard_map(
        shards,
        mesh=mesh,
        in_specs=placed,
        out_specs=(P("group", "tensor"), P("group", "tensor"), P("group", "tensor")),
        check_vma=False,
    )
```

```python
import functools
import math

import jax
import jax.numpy as jnp
from jax import lax
from jax.experimental import pallas as pl
from jax.experimental.pallas import tpu as pltpu
from jax.sharding import PartitionSpec as P

HEAD_DIM = 128
BLOCK = 32
ROWS = 128
SHARE = 8
SIDE = 4
EXPONENT = math.log2(math.e) / math.sqrt(HEAD_DIM)
ARRIVAL = (0, 1, 3, 2)
BACK = (0, 1, 3, 2)
VMEM = pl.BlockSpec(memory_space=pltpu.VMEM)
SMEM = pl.BlockSpec(memory_space=pltpu.SMEM)
F32 = jnp.float32
BF16 = jnp.bfloat16


def swap_cores():
    return [(i, i ^ 1) for i in range(2 * SIDE * SIDE)]


def along(phase, distance):
    pairs = []
    for y in range(SIDE):
        for z in range(SIDE):
            for core in range(2):
                if (core + phase) % 2 == 0:
                    to = (y, (z + distance) % SIDE)
                else:
                    to = ((y + distance) % SIDE, z)
                pairs.append(((y * SIDE + z) * 2 + core, (to[0] * SIDE + to[1]) * 2 + core))
    return pairs


def ring(distance):
    pairs = []
    for group in range(2 * SIDE * SIDE):
        for x in range(SIDE):
            to = (x + (distance if group % 2 == 0 else -distance)) % SIDE
            pairs.append((group * SIDE + x, group * SIDE + to))
    return pairs


def place():
    group = lax.axis_index("group")
    return lax.rem(group, 2), group // (2 * SIDE), lax.rem(group // 2, SIDE)


def sender(piece, slot):
    core, y, z = place()
    first, second = BACK[slot], BACK[piece]
    dy = jnp.where(core == 0, second, first)
    dz = jnp.where(core == 0, first, second)
    return lax.rem(y - dy + SIDE, SIDE) * SIDE + lax.rem(z - dz + SIDE, SIDE)


def cost(microseconds):
    return pl.CostEstimate(
        flops=int(microseconds * 1.1e9), bytes_accessed=int(microseconds * 3.5e6), transcendentals=0
    )


def heads_kernel(width, *refs):
    core, _, _ = place()
    arrays, (mine, give) = refs[:-2], refs[-2:]
    for which, target in ((core, mine), (1 - core, give)):
        at = 0
        for array in arrays:
            for i in range(0, width, HEAD_DIM):
                columns = pl.ds(pl.multiple_of(which * width + i, HEAD_DIM), HEAD_DIM)
                target[at : at + ROWS, :] = array[:, columns]
                at += ROWS


def heads(width, microseconds, *arrays):
    rows = len(arrays) * width // HEAD_DIM * ROWS
    tall = jax.ShapeDtypeStruct((rows, HEAD_DIM), BF16)
    return pl.pallas_call(
        functools.partial(heads_kernel, width),
        out_shape=(tall, tall),
        in_specs=[VMEM] * len(arrays),
        out_specs=(VMEM,) * 2,
        compiler_params=pltpu.CompilerParams(vmem_limit_bytes=4 << 20),
        cost_estimate=cost(microseconds),
        name="heads",
    )(*arrays)


def sent_from(step):
    core, _, _ = place()
    x = lax.axis_index("tensor")
    return lax.rem(jnp.where(core == 0, x - step, x + step) + SIDE, SIDE)


def near_kernel(*refs):
    pieces, weight, keys_out, values_out, rows = refs[:3], *refs[3:]
    size = pieces[0].shape[0]
    for i, piece in enumerate(pieces):
        rows[i * size : (i + 1) * size, :] = piece[...]
    keys = jnp.zeros(keys_out.shape, F32)
    values = jnp.zeros(keys_out.shape, F32)
    step = 1024
    for i in range(0, rows.shape[1], step):
        part = slice(i, i + step)
        keys += jnp.dot(rows[:, part], weight[0, part, :], preferred_element_type=F32)
        values += jnp.dot(rows[:, part], weight[1, part, :], preferred_element_type=F32)
    keys_out[...] = keys
    values_out[...] = values


def project_near(pieces, weight):
    count = sum(piece.shape[0] for piece in pieces)
    wide = jax.ShapeDtypeStruct((count, weight.shape[2]), F32)
    return pl.pallas_call(
        near_kernel,
        out_shape=(wide, wide),
        in_specs=[VMEM] * 4,
        out_specs=(VMEM,) * 2,
        scratch_shapes=[pltpu.VMEM((count, weight.shape[1]), BF16)],
        compiler_params=pltpu.CompilerParams(vmem_limit_bytes=24 << 20),
        cost_estimate=cost(20),
        name="project_near",
    )(*pieces, weight)


def far_kernel(piece, near_keys, near_values, weight, cosine, sine, *refs):
    new_keys, new_values, mine, give = refs
    size = piece.shape[0]
    keys = jnp.zeros((size, weight.shape[2]), F32)
    values = jnp.zeros((size, weight.shape[2]), F32)
    step = 1024
    for i in range(0, piece.shape[1], step):
        part = slice(i, i + step)
        keys += jnp.dot(piece[:, part], weight[0, part, :], preferred_element_type=F32)
        values += jnp.dot(piece[:, part], weight[1, part, :], preferred_element_type=F32)
    for i, back in enumerate(ARRIVAL):
        at = pl.ds(pl.multiple_of(sent_from(back) * size, size), size)
        part = slice(i * size, (i + 1) * size)
        last = i == len(ARRIVAL) - 1
        for h in range(2):
            head = slice(h * HEAD_DIM, (h + 1) * HEAD_DIM)
            key = keys[:, head] if last else near_keys[part, head]
            turned = key * cosine[at, :] + pltpu.roll(key, HEAD_DIM // 2, 1) * sine[at, :]
            new_keys[at, head] = turned.astype(BF16)
        value = values if last else near_values[part, :]
        new_values[at, :] = value.astype(BF16)
    core, _, _ = place()
    for which, target in ((core, mine), (1 - core, give)):
        head = pl.ds(pl.multiple_of(which * HEAD_DIM, HEAD_DIM), HEAD_DIM)
        target[0:ROWS, :] = new_keys[:, head]
        target[ROWS : 2 * ROWS, :] = new_values[:, head]


def project_far(piece, near_keys, near_values, weight, cosine, sine):
    wide = jax.ShapeDtypeStruct((ROWS, 2 * HEAD_DIM), BF16)
    tall = jax.ShapeDtypeStruct((2 * ROWS, HEAD_DIM), BF16)
    return pl.pallas_call(
        far_kernel,
        out_shape=(wide, wide, tall, tall),
        in_specs=[VMEM] * 6,
        out_specs=(VMEM,) * 4,
        compiler_params=pltpu.CompilerParams(vmem_limit_bytes=24 << 20),
        cost_estimate=cost(0.1),
        name="project_far",
    )(piece, near_keys, near_values, weight, cosine, sine)


def absorb(query, turned_keys, values, state, visible=None):
    top, den, num = state
    scores = jnp.dot(query, turned_keys, preferred_element_type=F32)
    if visible is not None:
        scores = jnp.where(visible, scores, -1e30)
    raised = jnp.maximum(top, jnp.max(scores, axis=1, keepdims=True))
    weights = [
        jnp.exp2((scores[:, i : i + HEAD_DIM] - raised) * EXPONENT)
        for i in range(0, scores.shape[1], HEAD_DIM)
    ]
    keep = jnp.exp2((top - raised) * EXPONENT)
    den = den * keep + functools.reduce(lambda a, b: a + b, weights)
    rounded = jnp.concatenate([w.astype(BF16) for w in weights], 1)
    num = num * keep + jnp.dot(rounded, values, preferred_element_type=F32)
    return raised, den, num


TILE = 1024


def tiles(own_queries, received):
    found = []
    for i in range(0, SHARE * ROWS, TILE):
        found.append((0, i, functools.partial(own_queries.__getitem__, slice(i, i + TILE))))
    for i in range(0, SHARE * ROWS, TILE):
        there = slice(i, i + TILE)
        found.append((1, SHARE * ROWS + i, functools.partial(received.__getitem__, there)))
    return found


STATE = jax.ShapeDtypeStruct((2 * SHARE * ROWS, HEAD_DIM), F32)


def cache_kernel(live_keys, kv_blocks, own_queries, received, *refs):
    pieces, states, (keys, values, turned) = refs[:4], refs[4:7], refs[7:]
    core, _, _ = place()
    at = jnp.int32(0)
    for piece in range(SIDE):
        for slot in range(SIDE):
            chip = sender(piece, slot)
            for half in range(2):
                group = chip * 2 + (core if half == 0 else 1 - core)
                row = slot * 4 * ROWS + half * 2 * ROWS
                there = pl.ds(pl.multiple_of(at, BLOCK), ROWS)
                keys[there, :] = pieces[piece][row : row + ROWS, :]
                values[there, :] = pieces[piece][row + ROWS : row + 2 * ROWS, :]
                at = at + kv_blocks[group] * BLOCK
    for i in range(0, live_keys, 256):
        turned[:, i : i + 256] = keys[i : i + 256, :].T
    for _, start, query in tiles(own_queries, received):
        zero = jnp.zeros((TILE, HEAD_DIM), F32)
        state = (jnp.full((TILE, HEAD_DIM), -1e30, F32), zero, zero)
        state = absorb(query(), turned[...], values[:live_keys, :], state)
        for ref, value in zip(states, state):
            ref[start : start + TILE, :] = value


def attend_cache(kv_blocks, own_queries, received, pieces, live_keys):
    held = pltpu.VMEM((live_keys + ROWS, HEAD_DIM), BF16)
    return pl.pallas_call(
        functools.partial(cache_kernel, live_keys),
        out_shape=(STATE,) * 3,
        in_specs=[SMEM] + [VMEM] * 6,
        out_specs=(VMEM,) * 3,
        scratch_shapes=[held, held, pltpu.VMEM((HEAD_DIM, live_keys), BF16)],
        compiler_params=pltpu.CompilerParams(vmem_limit_bytes=24 << 20),
        cost_estimate=cost(0.1),
        name="attend_cache",
    )(kv_blocks, own_queries, received, *pieces)


def new_kernel(which, last, own_queries, received, *refs):
    count = len(which)
    pieces, olds = refs[:count], refs[count : count + 3]
    outs, (turned, held), sums = refs[count + 3 :], refs[-5:-3], refs[-3:]
    core, y, z = place()
    size = 2 * ROWS
    if not last:
        sums = outs[:3]
    parts = tiles(own_queries, received)

    def visit(keys, values, sources, visible=None):
        for partner, start, query in parts:
            rows = slice(start, start + TILE)
            state = absorb(
                query(),
                keys,
                values,
                tuple(s[rows, :] for s in sources),
                visible(partner) if visible else None,
            )
            for s, value in zip(sums, state):
                s[rows, :] = value

    def block_of(ref, slot):
        base = slot * 4 * ROWS
        here = [slice(base + i * ROWS, base + (i + 1) * ROWS) for i in range(4)]
        keys = jnp.concatenate([ref[here[0], :], ref[here[2], :]], 0)
        return keys.T, jnp.concatenate([ref[here[1], :], ref[here[3], :]], 0)

    def causal(partner):
        shape = (TILE, size)
        row = lax.rem(lax.broadcasted_iota(jnp.int32, shape, 0), ROWS)
        row = row + jnp.where(core == partner, 0, ROWS)
        key = lax.broadcasted_iota(jnp.int32, shape, 1)
        key = jnp.where(core == 0, key, lax.rem(key + ROWS, size))
        return key <= row

    found = jnp.int32(0)
    for piece, ref in zip(which, pieces):
        for slot in range(SIDE):
            if piece == 0 and slot == 0:
                continue
            seen = sender(piece, slot) < y * SIDE + z

            def keep(ref=ref, slot=slot, found=found):
                there = pl.ds(pl.multiple_of(found * size, size), size)
                turned[:, there], held[there, :] = block_of(ref, slot)

            pl.when(seen)(keep)
            found = found + seen.astype(jnp.int32)

    def chunk(first, blocks, sources):
        there = pl.ds(pl.multiple_of(first * size, size), blocks * size)
        visit(turned[:, there], held[there, :], sources)

    def rest(first, sources):
        left = found - first

        def body(i, _):
            chunk(first + 4 * i, 4, sources)
            return 0

        lax.fori_loop(0, left // 4, body, 0)
        pl.when((left & 2) != 0)(lambda: chunk(first + (left // 4) * 4, 2, sources))
        pl.when((left & 1) != 0)(lambda: chunk(found - 1, 1, sources))

    if which[0] == 0:
        visit(*block_of(pieces[0], 0), olds, causal)
    else:
        for new, old in zip(sums, olds):
            new[...] = old[...]
    rest(jnp.int32(0), sums)

    if last:
        here, there = outs[:2]
        for partner, target in ((0, here), (1, there)):
            for head in range(SHARE):
                start = (partner * SHARE + head) * ROWS
                rows = slice(start, start + ROWS)
                den = jnp.sum(sums[1][rows, :], axis=1, keepdims=True)
                columns = slice(head * HEAD_DIM, (head + 1) * HEAD_DIM)
                target[:, columns] = (sums[2][rows, :] / den).astype(BF16)


def attend_new(own_queries, received, which, pieces, states, last):
    out = jax.ShapeDtypeStruct((ROWS, SHARE * HEAD_DIM), BF16)
    blocks = SIDE * len(which)
    total = pltpu.VMEM(STATE.shape if last else (8, HEAD_DIM), F32)
    return pl.pallas_call(
        functools.partial(new_kernel, which, last),
        out_shape=(out, out) if last else (STATE,) * 3,
        in_specs=[VMEM] * (2 + len(which) + 3),
        out_specs=(VMEM,) * (2 if last else 3),
        scratch_shapes=[
            pltpu.VMEM((HEAD_DIM, 2 * ROWS * blocks), BF16),
            pltpu.VMEM((2 * ROWS * blocks, HEAD_DIM), BF16),
            total,
            total,
            total,
        ],
        compiler_params=pltpu.CompilerParams(vmem_limit_bytes=24 << 20),
        cost_estimate=cost(0.1),
        name="attend_new_last" if last else "attend_new",
    )(own_queries, received, *pieces, *states)


def finish_kernel(here, other, keys, values, attended, keys_out, values_out, sems):
    core, _, _ = place()
    width = here.shape[1]

    def half(i):
        return attended.at[:, pl.ds(pl.multiple_of(i * width, width), width)]

    copies = [
        pltpu.make_async_copy(source, target, sems.at[i])
        for i, (source, target) in enumerate(
            ((here, half(core)), (other, half(1 - core)), (keys, keys_out), (values, values_out))
        )
    ]
    for copy in copies:
        copy.start()
    for copy in copies:
        copy.wait()


def finish(here, other, keys, values):
    rows, width = here.shape
    hbm = pl.BlockSpec(memory_space=pltpu.HBM)
    return pl.pallas_call(
        finish_kernel,
        out_shape=tuple(
            jax.ShapeDtypeStruct(shape, BF16) for shape in ((rows, 2 * width), keys.shape, values.shape)
        ),
        in_specs=[VMEM] * 4,
        out_specs=(hbm,) * 3,
        scratch_shapes=[pltpu.SemaphoreType.DMA((4,))],
        compiler_params=pltpu.CompilerParams(vmem_limit_bytes=4 << 20),
        cost_estimate=cost(0.1),
        name="finish",
    )(here, other, keys, values)


def after(value, *others):
    return lax.optimization_barrier((value, *others))[0]


def first_phase(block, *others):
    sent = [lax.ppermute(block, "group", along(0, d)) for d in (1, 3, 2)]
    return jnp.concatenate([after(block, *others) if others else block] + sent, 0)


def second_phase(joined):
    return [joined] + [lax.ppermute(joined, "group", along(1, d)) for d in (1, 3)]


def last_phase(joined, *others):
    return lax.ppermute(after(joined, *others), "group", along(1, 2))


def swapped(block):
    return lax.ppermute(block, "group", swap_cores())


def shards(queries, hidden_rows, kv_weight, cache_keys, cache_values, kv_blocks):
    group = lax.axis_index("group")
    core = lax.rem(group, 2)
    both = ("group", "tensor")
    ahead = lax.ppermute(hidden_rows, both, ring(1))
    mine, give = heads(HEAD_DIM, 0.1, cache_keys, cache_values)
    block = jnp.concatenate([mine, swapped(give)], 0)
    behind = lax.ppermute(after(hidden_rows, block), both, ring(3))
    joined = first_phase(block)
    own_queries, give_queries = heads(SHARE * HEAD_DIM, 5, after(queries, block))
    received = swapped(give_queries)
    far = lax.ppermute(after(ahead, own_queries), both, ring(1))
    cache = second_phase(joined)

    live_keys = cache_keys.shape[0] * kv_blocks.shape[0] // 2
    half = HEAD_DIM // 2
    positions = live_keys + group * ROWS + jnp.arange(ROWS, dtype=jnp.int32)
    freq = jnp.exp(jnp.arange(half, dtype=F32) * (-2.0 * math.log(500000.0) / HEAD_DIM))
    angle = positions.astype(F32)[:, None] * freq[None, :]
    cosine, sine = jnp.cos(angle), jnp.sin(angle)
    near_keys, near_values = project_near((hidden_rows, ahead, behind), kv_weight)
    cache.append(last_phase(joined, near_keys))
    new_keys, new_values, mine, give = project_far(
        after(far, received),
        near_keys,
        near_values,
        kv_weight,
        jnp.concatenate([cosine, cosine], 1),
        jnp.concatenate([-sine, sine], 1),
    )
    block = jnp.concatenate([mine, swapped(give)], 0)
    states = attend_cache(kv_blocks, after(own_queries, block), received, cache, live_keys)
    joined = first_phase(block, states[0])
    new = second_phase(joined)
    states = attend_new(own_queries, received, (0,), new[:1], states, False)
    new.append(last_phase(joined, states[0], new[1]))
    states = attend_new(own_queries, received, (1, 2), new[1:3], states, False)
    here, there = attend_new(own_queries, received, (3,), new[3:], states, True)
    other = swapped(there)
    return finish(here, other, new_keys, new_values)


def solution(mesh):
    placed = (
        P("group", "tensor"),
        P(("group", "tensor"), None),
        P(None, None, "tensor"),
        P("group", "tensor"),
        P("group", "tensor"),
        P(),
    )
    return jax.shard_map(
        shards,
        mesh=mesh,
        in_specs=placed,
        out_specs=(P("group", "tensor"), P("group", "tensor"), P("group", "tensor")),
        check_vma=False,
    )
```

```python
import functools
import math

import jax
import jax.numpy as jnp
from jax import lax
from jax.experimental import pallas as pl
from jax.experimental.pallas import tpu as pltpu
from jax.sharding import PartitionSpec as P

HEAD_DIM = 128
BLOCK = 32
ROWS = 128
SHARE = 8
SIDE = 4
EXPONENT = math.log2(math.e) / math.sqrt(HEAD_DIM)
ARRIVAL = (0, 1, 3, 2)
BACK = (0, 1, 3, 2)
VMEM = pl.BlockSpec(memory_space=pltpu.VMEM)
SMEM = pl.BlockSpec(memory_space=pltpu.SMEM)
F32 = jnp.float32
BF16 = jnp.bfloat16


def swap_cores():
    return [(i, i ^ 1) for i in range(2 * SIDE * SIDE)]


def along(phase, distance):
    pairs = []
    for y in range(SIDE):
        for z in range(SIDE):
            for core in range(2):
                if (core + phase) % 2 == 0:
                    to = (y, (z + distance) % SIDE)
                else:
                    to = ((y + distance) % SIDE, z)
                pairs.append(((y * SIDE + z) * 2 + core, (to[0] * SIDE + to[1]) * 2 + core))
    return pairs


def ring(distance):
    pairs = []
    for group in range(2 * SIDE * SIDE):
        for x in range(SIDE):
            to = (x + (distance if group % 2 == 0 else -distance)) % SIDE
            pairs.append((group * SIDE + x, group * SIDE + to))
    return pairs


def place():
    group = lax.axis_index("group")
    return lax.rem(group, 2), group // (2 * SIDE), lax.rem(group // 2, SIDE)


def sender(piece, slot):
    core, y, z = place()
    first, second = BACK[slot], BACK[piece]
    dy = jnp.where(core == 0, second, first)
    dz = jnp.where(core == 0, first, second)
    return lax.rem(y - dy + SIDE, SIDE) * SIDE + lax.rem(z - dz + SIDE, SIDE)


def cost(microseconds):
    return pl.CostEstimate(
        flops=int(microseconds * 1.1e9), bytes_accessed=int(microseconds * 3.5e6), transcendentals=0
    )


def heads_kernel(width, *refs):
    core, _, _ = place()
    arrays, (mine, give) = refs[:-2], refs[-2:]
    for which, target in ((core, mine), (1 - core, give)):
        at = 0
        for array in arrays:
            for i in range(0, width, HEAD_DIM):
                columns = pl.ds(pl.multiple_of(which * width + i, HEAD_DIM), HEAD_DIM)
                target[at : at + ROWS, :] = array[:, columns]
                at += ROWS


def heads(width, microseconds, *arrays):
    rows = len(arrays) * width // HEAD_DIM * ROWS
    tall = jax.ShapeDtypeStruct((rows, HEAD_DIM), BF16)
    return pl.pallas_call(
        functools.partial(heads_kernel, width),
        out_shape=(tall, tall),
        in_specs=[VMEM] * len(arrays),
        out_specs=(VMEM,) * 2,
        compiler_params=pltpu.CompilerParams(vmem_limit_bytes=4 << 20),
        cost_estimate=cost(microseconds),
        name="heads",
    )(*arrays)


def sent_from(step):
    core, _, _ = place()
    x = lax.axis_index("tensor")
    return lax.rem(jnp.where(core == 0, x - step, x + step) + SIDE, SIDE)


def near_kernel(*refs):
    pieces, weight, keys_out, values_out, rows = refs[:3], *refs[3:]
    size = pieces[0].shape[0]
    for i, piece in enumerate(pieces):
        rows[i * size : (i + 1) * size, :] = piece[...]
    keys = jnp.zeros(keys_out.shape, F32)
    values = jnp.zeros(keys_out.shape, F32)
    step = 1024
    for i in range(0, rows.shape[1], step):
        part = slice(i, i + step)
        keys += jnp.dot(rows[:, part], weight[0, part, :], preferred_element_type=F32)
        values += jnp.dot(rows[:, part], weight[1, part, :], preferred_element_type=F32)
    keys_out[...] = keys
    values_out[...] = values


def project_near(pieces, weight):
    count = sum(piece.shape[0] for piece in pieces)
    wide = jax.ShapeDtypeStruct((count, weight.shape[2]), F32)
    return pl.pallas_call(
        near_kernel,
        out_shape=(wide, wide),
        in_specs=[VMEM] * 4,
        out_specs=(VMEM,) * 2,
        scratch_shapes=[pltpu.VMEM((count, weight.shape[1]), BF16)],
        compiler_params=pltpu.CompilerParams(vmem_limit_bytes=24 << 20),
        cost_estimate=cost(20),
        name="project_near",
    )(*pieces, weight)


def far_kernel(piece, near_keys, near_values, weight, cosine, sine, *refs):
    new_keys, new_values, mine, give = refs
    size = piece.shape[0]
    keys = jnp.zeros((size, weight.shape[2]), F32)
    values = jnp.zeros((size, weight.shape[2]), F32)
    step = 1024
    for i in range(0, piece.shape[1], step):
        part = slice(i, i + step)
        keys += jnp.dot(piece[:, part], weight[0, part, :], preferred_element_type=F32)
        values += jnp.dot(piece[:, part], weight[1, part, :], preferred_element_type=F32)
    for i, back in enumerate(ARRIVAL):
        at = pl.ds(pl.multiple_of(sent_from(back) * size, size), size)
        part = slice(i * size, (i + 1) * size)
        last = i == len(ARRIVAL) - 1
        for h in range(2):
            head = slice(h * HEAD_DIM, (h + 1) * HEAD_DIM)
            key = keys[:, head] if last else near_keys[part, head]
            turned = key * cosine[at, :] + pltpu.roll(key, HEAD_DIM // 2, 1) * sine[at, :]
            new_keys[at, head] = turned.astype(BF16)
        value = values if last else near_values[part, :]
        new_values[at, :] = value.astype(BF16)
    core, _, _ = place()
    for which, target in ((core, mine), (1 - core, give)):
        head = pl.ds(pl.multiple_of(which * HEAD_DIM, HEAD_DIM), HEAD_DIM)
        target[0:ROWS, :] = new_keys[:, head]
        target[ROWS : 2 * ROWS, :] = new_values[:, head]


def project_far(piece, near_keys, near_values, weight, cosine, sine):
    wide = jax.ShapeDtypeStruct((ROWS, 2 * HEAD_DIM), BF16)
    tall = jax.ShapeDtypeStruct((2 * ROWS, HEAD_DIM), BF16)
    return pl.pallas_call(
        far_kernel,
        out_shape=(wide, wide, tall, tall),
        in_specs=[VMEM] * 6,
        out_specs=(VMEM,) * 4,
        compiler_params=pltpu.CompilerParams(vmem_limit_bytes=24 << 20),
        cost_estimate=cost(0.1),
        name="project_far",
    )(piece, near_keys, near_values, weight, cosine, sine)


def absorb(query, turned_keys, values, state, visible=None):
    top, den, num = state
    scores = jnp.dot(query, turned_keys, preferred_element_type=F32)
    if visible is not None:
        scores = jnp.where(visible, scores, -1e30)
    raised = jnp.maximum(top, jnp.max(scores, axis=1, keepdims=True))
    weights = [
        jnp.exp2((scores[:, i : i + HEAD_DIM] - raised) * EXPONENT)
        for i in range(0, scores.shape[1], HEAD_DIM)
    ]
    keep = jnp.exp2((top - raised) * EXPONENT)
    den = den * keep + functools.reduce(lambda a, b: a + b, weights)
    rounded = jnp.concatenate([w.astype(BF16) for w in weights], 1)
    num = num * keep + jnp.dot(rounded, values, preferred_element_type=F32)
    return raised, den, num


TILE = 1024


def tiles(own_queries, received):
    found = []
    for i in range(0, SHARE * ROWS, TILE):
        found.append((0, i, functools.partial(own_queries.__getitem__, slice(i, i + TILE))))
    for i in range(0, SHARE * ROWS, TILE):
        there = slice(i, i + TILE)
        found.append((1, SHARE * ROWS + i, functools.partial(received.__getitem__, there)))
    return found


STATE = jax.ShapeDtypeStruct((2 * SHARE * ROWS, HEAD_DIM), F32)


def cache_kernel(live_keys, kv_blocks, own_queries, received, *refs):
    pieces, states, (turned, rest), (keys, values) = refs[:4], refs[4:7], refs[7:9], refs[9:]
    first = live_keys - rest.shape[0]
    core, _, _ = place()
    at = jnp.int32(0)
    for piece in range(SIDE):
        for slot in range(SIDE):
            chip = sender(piece, slot)
            for half in range(2):
                group = chip * 2 + (core if half == 0 else 1 - core)
                row = slot * 4 * ROWS + half * 2 * ROWS
                there = pl.ds(pl.multiple_of(at, BLOCK), ROWS)
                keys[there, :] = pieces[piece][row : row + ROWS, :]
                values[there, :] = pieces[piece][row + ROWS : row + 2 * ROWS, :]
                at = at + kv_blocks[group] * BLOCK
    for i in range(0, live_keys, 256):
        turned[:, i : i + 256] = keys[i : i + 256, :].T
    rest[...] = values[first:live_keys, :]
    for _, start, query in tiles(own_queries, received):
        zero = jnp.zeros((TILE, HEAD_DIM), F32)
        state = (jnp.full((TILE, HEAD_DIM), -1e30, F32), zero, zero)
        state = absorb(query(), turned[:, :first], values[:first, :], state)
        for ref, value in zip(states, state):
            ref[start : start + TILE, :] = value


def attend_cache(kv_blocks, own_queries, received, pieces, live_keys, later):
    held = pltpu.VMEM((live_keys + ROWS, HEAD_DIM), BF16)
    return pl.pallas_call(
        functools.partial(cache_kernel, live_keys),
        out_shape=(STATE,) * 3
        + (
            jax.ShapeDtypeStruct((HEAD_DIM, live_keys), BF16),
            jax.ShapeDtypeStruct((later, HEAD_DIM), BF16),
        ),
        in_specs=[SMEM] + [VMEM] * 6,
        out_specs=(VMEM,) * 5,
        scratch_shapes=[held, held],
        compiler_params=pltpu.CompilerParams(vmem_limit_bytes=24 << 20),
        cost_estimate=cost(0.1),
        name="attend_cache",
    )(kv_blocks, own_queries, received, *pieces)


def later_kernel(own_queries, received, turned, values, *refs):
    olds, states = refs[:3], refs[3:]
    first = turned.shape[1] - values.shape[0]
    for _, start, query in tiles(own_queries, received):
        rows = slice(start, start + TILE)
        state = tuple(old[rows, :] for old in olds)
        state = absorb(query(), turned[:, first:], values[...], state)
        for ref, value in zip(states, state):
            ref[rows, :] = value


def attend_later(own_queries, received, turned, values, states):
    return pl.pallas_call(
        later_kernel,
        out_shape=(STATE,) * 3,
        in_specs=[VMEM] * 7,
        out_specs=(VMEM,) * 3,
        compiler_params=pltpu.CompilerParams(vmem_limit_bytes=24 << 20),
        cost_estimate=cost(0.1),
        name="attend_later",
    )(own_queries, received, turned, values, *states)


def new_kernel(which, last, own_queries, received, *refs):
    count = len(which)
    pieces, olds = refs[:count], refs[count : count + 3]
    outs, (turned, held), sums = refs[count + 3 :], refs[-5:-3], refs[-3:]
    core, y, z = place()
    size = 2 * ROWS
    if not last:
        sums = outs[:3]
    parts = tiles(own_queries, received)

    def visit(keys, values, sources, visible=None):
        for partner, start, query in parts:
            rows = slice(start, start + TILE)
            state = absorb(
                query(),
                keys,
                values,
                tuple(s[rows, :] for s in sources),
                visible(partner) if visible else None,
            )
            for s, value in zip(sums, state):
                s[rows, :] = value

    def block_of(ref, slot):
        base = slot * 4 * ROWS
        here = [slice(base + i * ROWS, base + (i + 1) * ROWS) for i in range(4)]
        keys = jnp.concatenate([ref[here[0], :], ref[here[2], :]], 0)
        return keys.T, jnp.concatenate([ref[here[1], :], ref[here[3], :]], 0)

    def causal(partner):
        shape = (TILE, size)
        row = lax.rem(lax.broadcasted_iota(jnp.int32, shape, 0), ROWS)
        row = row + jnp.where(core == partner, 0, ROWS)
        key = lax.broadcasted_iota(jnp.int32, shape, 1)
        key = jnp.where(core == 0, key, lax.rem(key + ROWS, size))
        return key <= row

    found = jnp.int32(0)
    for piece, ref in zip(which, pieces):
        for slot in range(SIDE):
            if piece == 0 and slot == 0:
                continue
            seen = sender(piece, slot) < y * SIDE + z

            def keep(ref=ref, slot=slot, found=found):
                there = pl.ds(pl.multiple_of(found * size, size), size)
                turned[:, there], held[there, :] = block_of(ref, slot)

            pl.when(seen)(keep)
            found = found + seen.astype(jnp.int32)

    def chunk(first, blocks, sources):
        there = pl.ds(pl.multiple_of(first * size, size), blocks * size)
        visit(turned[:, there], held[there, :], sources)

    def rest(first, sources):
        left = found - first

        def body(i, _):
            chunk(first + 4 * i, 4, sources)
            return 0

        lax.fori_loop(0, left // 4, body, 0)
        pl.when((left & 2) != 0)(lambda: chunk(first + (left // 4) * 4, 2, sources))
        pl.when((left & 1) != 0)(lambda: chunk(found - 1, 1, sources))

    if which[0] == 0:
        visit(*block_of(pieces[0], 0), olds, causal)
    else:
        for new, old in zip(sums, olds):
            new[...] = old[...]
    rest(jnp.int32(0), sums)

    if last:
        here, there = outs[:2]
        for partner, target in ((0, here), (1, there)):
            for head in range(SHARE):
                start = (partner * SHARE + head) * ROWS
                rows = slice(start, start + ROWS)
                den = jnp.sum(sums[1][rows, :], axis=1, keepdims=True)
                columns = slice(head * HEAD_DIM, (head + 1) * HEAD_DIM)
                target[:, columns] = (sums[2][rows, :] / den).astype(BF16)


def attend_new(own_queries, received, which, pieces, states, last):
    out = jax.ShapeDtypeStruct((ROWS, SHARE * HEAD_DIM), BF16)
    blocks = SIDE * len(which)
    total = pltpu.VMEM(STATE.shape if last else (8, HEAD_DIM), F32)
    return pl.pallas_call(
        functools.partial(new_kernel, which, last),
        out_shape=(out, out) if last else (STATE,) * 3,
        in_specs=[VMEM] * (2 + len(which) + 3),
        out_specs=(VMEM,) * (2 if last else 3),
        scratch_shapes=[
            pltpu.VMEM((HEAD_DIM, 2 * ROWS * blocks), BF16),
            pltpu.VMEM((2 * ROWS * blocks, HEAD_DIM), BF16),
            total,
            total,
            total,
        ],
        compiler_params=pltpu.CompilerParams(vmem_limit_bytes=24 << 20),
        cost_estimate=cost(0.1),
        name="attend_new_last" if last else "attend_new",
    )(own_queries, received, *pieces, *states)


def finish_kernel(here, other, keys, values, attended, keys_out, values_out, sems):
    core, _, _ = place()
    width = here.shape[1]

    def half(i):
        return attended.at[:, pl.ds(pl.multiple_of(i * width, width), width)]

    copies = [
        pltpu.make_async_copy(source, target, sems.at[i])
        for i, (source, target) in enumerate(
            ((here, half(core)), (other, half(1 - core)), (keys, keys_out), (values, values_out))
        )
    ]
    for copy in copies:
        copy.start()
    for copy in copies:
        copy.wait()


def finish(here, other, keys, values):
    rows, width = here.shape
    hbm = pl.BlockSpec(memory_space=pltpu.HBM)
    return pl.pallas_call(
        finish_kernel,
        out_shape=tuple(
            jax.ShapeDtypeStruct(shape, BF16) for shape in ((rows, 2 * width), keys.shape, values.shape)
        ),
        in_specs=[VMEM] * 4,
        out_specs=(hbm,) * 3,
        scratch_shapes=[pltpu.SemaphoreType.DMA((4,))],
        compiler_params=pltpu.CompilerParams(vmem_limit_bytes=4 << 20),
        cost_estimate=cost(0.1),
        name="finish",
    )(here, other, keys, values)


def after(value, *others):
    return lax.optimization_barrier((value, *others))[0]


def first_phase(block, *others):
    sent = [lax.ppermute(block, "group", along(0, d)) for d in (1, 3, 2)]
    return jnp.concatenate([after(block, *others) if others else block] + sent, 0)


def second_phase(joined):
    return [joined] + [lax.ppermute(joined, "group", along(1, d)) for d in (1, 3)]


def last_phase(joined, *others):
    return lax.ppermute(after(joined, *others), "group", along(1, 2))


def swapped(block):
    return lax.ppermute(block, "group", swap_cores())


def shards(queries, hidden_rows, kv_weight, cache_keys, cache_values, kv_blocks):
    group = lax.axis_index("group")
    core = lax.rem(group, 2)
    both = ("group", "tensor")
    ahead = lax.ppermute(hidden_rows, both, ring(1))
    mine, give = heads(HEAD_DIM, 0.1, cache_keys, cache_values)
    block = jnp.concatenate([mine, swapped(give)], 0)
    behind = lax.ppermute(after(hidden_rows, block), both, ring(3))
    joined = first_phase(block)
    own_queries, give_queries = heads(SHARE * HEAD_DIM, 5, after(queries, block))
    received = swapped(give_queries)
    far = lax.ppermute(after(ahead, own_queries), both, ring(1))
    cache = second_phase(joined)

    live_keys = cache_keys.shape[0] * kv_blocks.shape[0] // 2
    half = HEAD_DIM // 2
    positions = live_keys + group * ROWS + jnp.arange(ROWS, dtype=jnp.int32)
    freq = jnp.exp(jnp.arange(half, dtype=F32) * (-2.0 * math.log(500000.0) / HEAD_DIM))
    angle = positions.astype(F32)[:, None] * freq[None, :]
    cosine, sine = jnp.cos(angle), jnp.sin(angle)
    near_keys, near_values = project_near((hidden_rows, ahead, behind), kv_weight)
    cache.append(last_phase(joined, near_keys))
    new_keys, new_values, mine, give = project_far(
        after(far, received),
        near_keys,
        near_values,
        kv_weight,
        jnp.concatenate([cosine, cosine], 1),
        jnp.concatenate([-sine, sine], 1),
    )
    block = jnp.concatenate([mine, swapped(give)], 0)
    *states, turned, values = attend_cache(
        kv_blocks, after(own_queries, block), received, cache, live_keys, live_keys // 2
    )
    joined = first_phase(block, states[0])
    new = second_phase(joined)
    states = attend_new(own_queries, received, (0,), new[:1], states, False)
    states = attend_later(own_queries, received, turned, values, states)
    new.append(last_phase(joined, states[0], new[1]))
    states = attend_new(own_queries, received, (1, 2), new[1:3], states, False)
    here, there = attend_new(own_queries, received, (3,), new[3:], states, True)
    other = swapped(there)
    return finish(here, other, new_keys, new_values)


def solution(mesh):
    placed = (
        P("group", "tensor"),
        P(("group", "tensor"), None),
        P(None, None, "tensor"),
        P("group", "tensor"),
        P("group", "tensor"),
        P(),
    )
    return jax.shard_map(
        shards,
        mesh=mesh,
        in_specs=placed,
        out_specs=(P("group", "tensor"), P("group", "tensor"), P("group", "tensor")),
        check_vma=False,
    )
```

```python
import functools
import math

import jax
import jax.numpy as jnp
from jax import lax
from jax.experimental import pallas as pl
from jax.experimental.pallas import tpu as pltpu
from jax.sharding import PartitionSpec as P

HEAD_DIM = 128
BLOCK = 32
ROWS = 128
SHARE = 8
SIDE = 4
EXPONENT = math.log2(math.e) / math.sqrt(HEAD_DIM)
ARRIVAL = (0, 1, 3, 2)
BACK = (0, 1, 3, 2)
VMEM = pl.BlockSpec(memory_space=pltpu.VMEM)
SMEM = pl.BlockSpec(memory_space=pltpu.SMEM)
F32 = jnp.float32
BF16 = jnp.bfloat16


def swap_cores():
    return [(i, i ^ 1) for i in range(2 * SIDE * SIDE)]


def along(phase, distance):
    pairs = []
    for y in range(SIDE):
        for z in range(SIDE):
            for core in range(2):
                if (core + phase) % 2 == 0:
                    to = (y, (z + distance) % SIDE)
                else:
                    to = ((y + distance) % SIDE, z)
                pairs.append(((y * SIDE + z) * 2 + core, (to[0] * SIDE + to[1]) * 2 + core))
    return pairs


def ring(distance):
    pairs = []
    for group in range(2 * SIDE * SIDE):
        for x in range(SIDE):
            to = (x + (distance if group % 2 == 0 else -distance)) % SIDE
            pairs.append((group * SIDE + x, group * SIDE + to))
    return pairs


def place():
    group = lax.axis_index("group")
    return lax.rem(group, 2), group // (2 * SIDE), lax.rem(group // 2, SIDE)


def sender(piece, slot):
    core, y, z = place()
    first, second = BACK[slot], BACK[piece]
    dy = jnp.where(core == 0, second, first)
    dz = jnp.where(core == 0, first, second)
    return lax.rem(y - dy + SIDE, SIDE) * SIDE + lax.rem(z - dz + SIDE, SIDE)


def cost(microseconds):
    return pl.CostEstimate(
        flops=int(microseconds * 1.1e9), bytes_accessed=int(microseconds * 3.5e6), transcendentals=0
    )


def heads_kernel(width, *refs):
    core, _, _ = place()
    arrays, (mine, give) = refs[:-2], refs[-2:]
    for which, target in ((core, mine), (1 - core, give)):
        at = 0
        for array in arrays:
            for i in range(0, width, HEAD_DIM):
                columns = pl.ds(pl.multiple_of(which * width + i, HEAD_DIM), HEAD_DIM)
                target[at : at + ROWS, :] = array[:, columns]
                at += ROWS


def heads(width, microseconds, *arrays):
    rows = len(arrays) * width // HEAD_DIM * ROWS
    tall = jax.ShapeDtypeStruct((rows, HEAD_DIM), BF16)
    return pl.pallas_call(
        functools.partial(heads_kernel, width),
        out_shape=(tall, tall),
        in_specs=[VMEM] * len(arrays),
        out_specs=(VMEM,) * 2,
        compiler_params=pltpu.CompilerParams(vmem_limit_bytes=4 << 20),
        cost_estimate=cost(microseconds),
        name="heads",
    )(*arrays)


def sent_from(step):
    core, _, _ = place()
    x = lax.axis_index("tensor")
    return lax.rem(jnp.where(core == 0, x - step, x + step) + SIDE, SIDE)


def near_kernel(*refs):
    pieces, weight, keys_out, values_out, rows = refs[:3], *refs[3:]
    size = pieces[0].shape[0]
    for i, piece in enumerate(pieces):
        rows[i * size : (i + 1) * size, :] = piece[...]
    keys = jnp.zeros(keys_out.shape, F32)
    values = jnp.zeros(keys_out.shape, F32)
    step = 1024
    for i in range(0, rows.shape[1], step):
        part = slice(i, i + step)
        keys += jnp.dot(rows[:, part], weight[0, part, :], preferred_element_type=F32)
        values += jnp.dot(rows[:, part], weight[1, part, :], preferred_element_type=F32)
    keys_out[...] = keys
    values_out[...] = values


def project_near(pieces, weight):
    count = sum(piece.shape[0] for piece in pieces)
    wide = jax.ShapeDtypeStruct((count, weight.shape[2]), F32)
    return pl.pallas_call(
        near_kernel,
        out_shape=(wide, wide),
        in_specs=[VMEM] * 4,
        out_specs=(VMEM,) * 2,
        scratch_shapes=[pltpu.VMEM((count, weight.shape[1]), BF16)],
        compiler_params=pltpu.CompilerParams(vmem_limit_bytes=24 << 20),
        cost_estimate=cost(20),
        name="project_near",
    )(*pieces, weight)


def far_kernel(piece, near_keys, near_values, weight, cosine, sine, *refs):
    new_keys, new_values, mine, give = refs
    size = piece.shape[0]
    keys = jnp.zeros((size, weight.shape[2]), F32)
    values = jnp.zeros((size, weight.shape[2]), F32)
    step = 1024
    for i in range(0, piece.shape[1], step):
        part = slice(i, i + step)
        keys += jnp.dot(piece[:, part], weight[0, part, :], preferred_element_type=F32)
        values += jnp.dot(piece[:, part], weight[1, part, :], preferred_element_type=F32)
    for i, back in enumerate(ARRIVAL):
        at = pl.ds(pl.multiple_of(sent_from(back) * size, size), size)
        part = slice(i * size, (i + 1) * size)
        last = i == len(ARRIVAL) - 1
        for h in range(2):
            head = slice(h * HEAD_DIM, (h + 1) * HEAD_DIM)
            key = keys[:, head] if last else near_keys[part, head]
            turned = key * cosine[at, :] + pltpu.roll(key, HEAD_DIM // 2, 1) * sine[at, :]
            new_keys[at, head] = turned.astype(BF16)
        value = values if last else near_values[part, :]
        new_values[at, :] = value.astype(BF16)
    core, _, _ = place()
    for which, target in ((core, mine), (1 - core, give)):
        head = pl.ds(pl.multiple_of(which * HEAD_DIM, HEAD_DIM), HEAD_DIM)
        target[0:ROWS, :] = new_keys[:, head]
        target[ROWS : 2 * ROWS, :] = new_values[:, head]


def project_far(piece, near_keys, near_values, weight, cosine, sine):
    wide = jax.ShapeDtypeStruct((ROWS, 2 * HEAD_DIM), BF16)
    tall = jax.ShapeDtypeStruct((2 * ROWS, HEAD_DIM), BF16)
    return pl.pallas_call(
        far_kernel,
        out_shape=(wide, wide, tall, tall),
        in_specs=[VMEM] * 6,
        out_specs=(VMEM,) * 4,
        compiler_params=pltpu.CompilerParams(vmem_limit_bytes=24 << 20),
        cost_estimate=cost(0.1),
        name="project_far",
    )(piece, near_keys, near_values, weight, cosine, sine)


def absorb(query, turned_keys, values, state, visible=None):
    top, den, num = state
    scores = jnp.dot(query, turned_keys, preferred_element_type=F32)
    if visible is not None:
        scores = jnp.where(visible, scores, -1e30)
    raised = jnp.maximum(top, jnp.max(scores, axis=1, keepdims=True))
    weights = [
        jnp.exp2((scores[:, i : i + HEAD_DIM] - raised) * EXPONENT)
        for i in range(0, scores.shape[1], HEAD_DIM)
    ]
    keep = jnp.exp2((top - raised) * EXPONENT)
    den = den * keep + functools.reduce(lambda a, b: a + b, weights)
    rounded = jnp.concatenate([w.astype(BF16) for w in weights], 1)
    num = num * keep + jnp.dot(rounded, values, preferred_element_type=F32)
    return raised, den, num


TILE = 1024


def tiles(own_queries, received):
    found = []
    for i in range(0, SHARE * ROWS, TILE):
        found.append((0, i, functools.partial(own_queries.__getitem__, slice(i, i + TILE))))
    for i in range(0, SHARE * ROWS, TILE):
        there = slice(i, i + TILE)
        found.append((1, SHARE * ROWS + i, functools.partial(received.__getitem__, there)))
    return found


STATE = jax.ShapeDtypeStruct((2 * SHARE * ROWS, HEAD_DIM), F32)


def cache_kernel(live_keys, kv_blocks, own_queries, received, *refs):
    pieces, states, (turned, rest), (keys, values) = refs[:4], refs[4:7], refs[7:9], refs[9:]
    first = live_keys - rest.shape[0]
    core, _, _ = place()
    at = jnp.int32(0)
    for piece in range(SIDE):
        for slot in range(SIDE):
            chip = sender(piece, slot)
            for half in range(2):
                group = chip * 2 + (core if half == 0 else 1 - core)
                row = slot * 4 * ROWS + half * 2 * ROWS
                there = pl.ds(pl.multiple_of(at, BLOCK), ROWS)
                keys[there, :] = pieces[piece][row : row + ROWS, :]
                values[there, :] = pieces[piece][row + ROWS : row + 2 * ROWS, :]
                at = at + kv_blocks[group] * BLOCK
    for i in range(0, live_keys, 256):
        turned[:, i : i + 256] = keys[i : i + 256, :].T
    rest[...] = values[first:live_keys, :]
    for _, start, query in tiles(own_queries, received):
        zero = jnp.zeros((TILE, HEAD_DIM), F32)
        state = (jnp.full((TILE, HEAD_DIM), -1e30, F32), zero, zero)
        state = absorb(query(), turned[:, :first], values[:first, :], state)
        for ref, value in zip(states, state):
            ref[start : start + TILE, :] = value


def attend_cache(kv_blocks, own_queries, received, pieces, live_keys, later):
    held = pltpu.VMEM((live_keys + ROWS, HEAD_DIM), BF16)
    return pl.pallas_call(
        functools.partial(cache_kernel, live_keys),
        out_shape=(STATE,) * 3
        + (
            jax.ShapeDtypeStruct((HEAD_DIM, live_keys), BF16),
            jax.ShapeDtypeStruct((later, HEAD_DIM), BF16),
        ),
        in_specs=[SMEM] + [VMEM] * 6,
        out_specs=(VMEM,) * 5,
        scratch_shapes=[held, held],
        compiler_params=pltpu.CompilerParams(vmem_limit_bytes=24 << 20),
        cost_estimate=cost(0.1),
        name="attend_cache",
    )(kv_blocks, own_queries, received, *pieces)


def later_kernel(own_queries, received, turned, values, *refs):
    olds, states = refs[:3], refs[3:]
    first = turned.shape[1] - values.shape[0]
    for _, start, query in tiles(own_queries, received):
        rows = slice(start, start + TILE)
        state = tuple(old[rows, :] for old in olds)
        state = absorb(query(), turned[:, first:], values[...], state)
        for ref, value in zip(states, state):
            ref[rows, :] = value


def attend_later(own_queries, received, turned, values, states):
    return pl.pallas_call(
        later_kernel,
        out_shape=(STATE,) * 3,
        in_specs=[VMEM] * 7,
        out_specs=(VMEM,) * 3,
        compiler_params=pltpu.CompilerParams(vmem_limit_bytes=24 << 20),
        cost_estimate=cost(0.1),
        name="attend_later",
    )(own_queries, received, turned, values, *states)


def new_kernel(which, last, own_queries, received, *refs):
    count = len(which)
    pieces, olds = refs[:count], refs[count : count + 3]
    outs, (turned, held), sums = refs[count + 3 :], refs[-5:-3], refs[-3:]
    core, y, z = place()
    size = 2 * ROWS
    if not last:
        sums = outs[:3]
    parts = tiles(own_queries, received)

    def visit(keys, values, sources, visible=None):
        for partner, start, query in parts:
            rows = slice(start, start + TILE)
            state = absorb(
                query(),
                keys,
                values,
                tuple(s[rows, :] for s in sources),
                visible(partner) if visible else None,
            )
            for s, value in zip(sums, state):
                s[rows, :] = value

    def block_of(ref, slot):
        base = slot * 4 * ROWS
        here = [slice(base + i * ROWS, base + (i + 1) * ROWS) for i in range(4)]
        keys = jnp.concatenate([ref[here[0], :], ref[here[2], :]], 0)
        return keys.T, jnp.concatenate([ref[here[1], :], ref[here[3], :]], 0)

    def causal(partner):
        shape = (TILE, size)
        row = lax.rem(lax.broadcasted_iota(jnp.int32, shape, 0), ROWS)
        row = row + jnp.where(core == partner, 0, ROWS)
        key = lax.broadcasted_iota(jnp.int32, shape, 1)
        key = jnp.where(core == 0, key, lax.rem(key + ROWS, size))
        return key <= row

    found = jnp.int32(0)
    for piece, ref in zip(which, pieces):
        for slot in range(SIDE):
            if piece == 0 and slot == 0:
                continue
            seen = sender(piece, slot) < y * SIDE + z

            def keep(ref=ref, slot=slot, found=found):
                there = pl.ds(pl.multiple_of(found * size, size), size)
                turned[:, there], held[there, :] = block_of(ref, slot)

            pl.when(seen)(keep)
            found = found + seen.astype(jnp.int32)

    def chunk(first, blocks, sources):
        there = pl.ds(pl.multiple_of(first * size, size), blocks * size)
        visit(turned[:, there], held[there, :], sources)

    def rest(first, sources):
        left = found - first
        most = 2 * SIDE
        whole = len(which) > 1
        if whole:
            pl.when(left == most)(lambda: chunk(first, most, sources))
            left = jnp.where(left == most, 0, left)

        def body(i, _):
            chunk(first + 4 * i, 4, sources)
            return 0

        lax.fori_loop(0, left // 4, body, 0)
        pl.when((left & 2) != 0)(lambda: chunk(first + (left // 4) * 4, 2, sources))
        pl.when((left & 1) != 0)(lambda: chunk(found - 1, 1, sources))

    if which[0] == 0:
        visit(*block_of(pieces[0], 0), olds, causal)
    else:
        for new, old in zip(sums, olds):
            new[...] = old[...]
    rest(jnp.int32(0), sums)

    if last:
        here, there = outs[:2]
        for partner, target in ((0, here), (1, there)):
            for head in range(SHARE):
                start = (partner * SHARE + head) * ROWS
                rows = slice(start, start + ROWS)
                den = jnp.sum(sums[1][rows, :], axis=1, keepdims=True)
                columns = slice(head * HEAD_DIM, (head + 1) * HEAD_DIM)
                target[:, columns] = (sums[2][rows, :] / den).astype(BF16)


def attend_new(own_queries, received, which, pieces, states, last):
    out = jax.ShapeDtypeStruct((ROWS, SHARE * HEAD_DIM), BF16)
    blocks = SIDE * len(which)
    total = pltpu.VMEM(STATE.shape if last else (8, HEAD_DIM), F32)
    return pl.pallas_call(
        functools.partial(new_kernel, which, last),
        out_shape=(out, out) if last else (STATE,) * 3,
        in_specs=[VMEM] * (2 + len(which) + 3),
        out_specs=(VMEM,) * (2 if last else 3),
        scratch_shapes=[
            pltpu.VMEM((HEAD_DIM, 2 * ROWS * blocks), BF16),
            pltpu.VMEM((2 * ROWS * blocks, HEAD_DIM), BF16),
            total,
            total,
            total,
        ],
        compiler_params=pltpu.CompilerParams(vmem_limit_bytes=24 << 20),
        cost_estimate=cost(0.1),
        name="attend_new_last" if last else "attend_new",
    )(own_queries, received, *pieces, *states)


def finish_kernel(here, other, keys, values, attended, keys_out, values_out, sems):
    core, _, _ = place()
    width = here.shape[1]

    def half(i):
        return attended.at[:, pl.ds(pl.multiple_of(i * width, width), width)]

    copies = [
        pltpu.make_async_copy(source, target, sems.at[i])
        for i, (source, target) in enumerate(
            ((here, half(core)), (other, half(1 - core)), (keys, keys_out), (values, values_out))
        )
    ]
    for copy in copies:
        copy.start()
    for copy in copies:
        copy.wait()


def finish(here, other, keys, values):
    rows, width = here.shape
    hbm = pl.BlockSpec(memory_space=pltpu.HBM)
    return pl.pallas_call(
        finish_kernel,
        out_shape=tuple(
            jax.ShapeDtypeStruct(shape, BF16) for shape in ((rows, 2 * width), keys.shape, values.shape)
        ),
        in_specs=[VMEM] * 4,
        out_specs=(hbm,) * 3,
        scratch_shapes=[pltpu.SemaphoreType.DMA((4,))],
        compiler_params=pltpu.CompilerParams(vmem_limit_bytes=4 << 20),
        cost_estimate=cost(0.1),
        name="finish",
    )(here, other, keys, values)


def after(value, *others):
    return lax.optimization_barrier((value, *others))[0]


def first_phase(block, *others):
    sent = [lax.ppermute(block, "group", along(0, d)) for d in (1, 3, 2)]
    return jnp.concatenate([after(block, *others) if others else block] + sent, 0)


def second_phase(joined):
    return [joined] + [lax.ppermute(joined, "group", along(1, d)) for d in (1, 3)]


def last_phase(joined, *others):
    return lax.ppermute(after(joined, *others), "group", along(1, 2))


def swapped(block):
    return lax.ppermute(block, "group", swap_cores())


def shards(queries, hidden_rows, kv_weight, cache_keys, cache_values, kv_blocks):
    group = lax.axis_index("group")
    core = lax.rem(group, 2)
    both = ("group", "tensor")
    ahead = lax.ppermute(hidden_rows, both, ring(1))
    mine, give = heads(HEAD_DIM, 0.1, cache_keys, cache_values)
    block = jnp.concatenate([mine, swapped(give)], 0)
    behind = lax.ppermute(after(hidden_rows, block), both, ring(3))
    joined = first_phase(block)
    own_queries, give_queries = heads(SHARE * HEAD_DIM, 5, after(queries, block))
    received = swapped(give_queries)
    far = lax.ppermute(after(ahead, own_queries), both, ring(1))
    cache = second_phase(joined)

    live_keys = cache_keys.shape[0] * kv_blocks.shape[0] // 2
    half = HEAD_DIM // 2
    positions = live_keys + group * ROWS + jnp.arange(ROWS, dtype=jnp.int32)
    freq = jnp.exp(jnp.arange(half, dtype=F32) * (-2.0 * math.log(500000.0) / HEAD_DIM))
    angle = positions.astype(F32)[:, None] * freq[None, :]
    cosine, sine = jnp.cos(angle), jnp.sin(angle)
    near_keys, near_values = project_near((hidden_rows, ahead, behind), kv_weight)
    cache.append(last_phase(joined, near_keys))
    new_keys, new_values, mine, give = project_far(
        after(far, received),
        near_keys,
        near_values,
        kv_weight,
        jnp.concatenate([cosine, cosine], 1),
        jnp.concatenate([-sine, sine], 1),
    )
    block = jnp.concatenate([mine, swapped(give)], 0)
    *states, turned, values = attend_cache(
        kv_blocks, after(own_queries, block), received, cache, live_keys, live_keys // 8 * 5
    )
    joined = first_phase(block, states[0])
    new = second_phase(joined)
    states = attend_new(own_queries, received, (0,), new[:1], states, False)
    states = attend_later(own_queries, received, turned, values, states)
    new.append(last_phase(joined, states[0], new[1]))
    states = attend_new(own_queries, received, (1, 2), new[1:3], states, False)
    here, there = attend_new(own_queries, received, (3,), new[3:], states, True)
    other = swapped(there)
    return finish(here, other, new_keys, new_values)


def solution(mesh):
    placed = (
        P("group", "tensor"),
        P(("group", "tensor"), None),
        P(None, None, "tensor"),
        P("group", "tensor"),
        P("group", "tensor"),
        P(),
    )
    return jax.shard_map(
        shards,
        mesh=mesh,
        in_specs=placed,
        out_specs=(P("group", "tensor"), P("group", "tensor"), P("group", "tensor")),
        check_vma=False,
    )
```

```python
import functools
import math

import jax
import jax.numpy as jnp
from jax import lax
from jax.experimental import pallas as pl
from jax.experimental.pallas import tpu as pltpu
from jax.sharding import PartitionSpec as P

HEAD_DIM = 128
BLOCK = 32
ROWS = 128
SHARE = 8
SIDE = 4
EXPONENT = math.log2(math.e) / math.sqrt(HEAD_DIM)
ARRIVAL = (0, 1, 3, 2)
BACK = (0, 1, 3, 2)
VMEM = pl.BlockSpec(memory_space=pltpu.VMEM)
SMEM = pl.BlockSpec(memory_space=pltpu.SMEM)
F32 = jnp.float32
BF16 = jnp.bfloat16


def swap_cores():
    return [(i, i ^ 1) for i in range(2 * SIDE * SIDE)]


def along(phase, distance):
    pairs = []
    for y in range(SIDE):
        for z in range(SIDE):
            for core in range(2):
                if (core + phase) % 2 == 0:
                    to = (y, (z + distance) % SIDE)
                else:
                    to = ((y + distance) % SIDE, z)
                pairs.append(((y * SIDE + z) * 2 + core, (to[0] * SIDE + to[1]) * 2 + core))
    return pairs


def ring(distance):
    pairs = []
    for group in range(2 * SIDE * SIDE):
        for x in range(SIDE):
            to = (x + (distance if group % 2 == 0 else -distance)) % SIDE
            pairs.append((group * SIDE + x, group * SIDE + to))
    return pairs


def place():
    group = lax.axis_index("group")
    return lax.rem(group, 2), group // (2 * SIDE), lax.rem(group // 2, SIDE)


def sender(piece, slot):
    core, y, z = place()
    first, second = BACK[slot], BACK[piece]
    dy = jnp.where(core == 0, second, first)
    dz = jnp.where(core == 0, first, second)
    return lax.rem(y - dy + SIDE, SIDE) * SIDE + lax.rem(z - dz + SIDE, SIDE)


def cost(microseconds):
    return pl.CostEstimate(
        flops=int(microseconds * 1.1e9), bytes_accessed=int(microseconds * 3.5e6), transcendentals=0
    )


def heads_kernel(width, *refs):
    core, _, _ = place()
    arrays, (mine, give) = refs[:-2], refs[-2:]
    for which, target in ((core, mine), (1 - core, give)):
        at = 0
        for array in arrays:
            for i in range(0, width, HEAD_DIM):
                columns = pl.ds(pl.multiple_of(which * width + i, HEAD_DIM), HEAD_DIM)
                target[at : at + ROWS, :] = array[:, columns]
                at += ROWS


def heads(width, microseconds, *arrays):
    rows = len(arrays) * width // HEAD_DIM * ROWS
    tall = jax.ShapeDtypeStruct((rows, HEAD_DIM), BF16)
    return pl.pallas_call(
        functools.partial(heads_kernel, width),
        out_shape=(tall, tall),
        in_specs=[VMEM] * len(arrays),
        out_specs=(VMEM,) * 2,
        compiler_params=pltpu.CompilerParams(vmem_limit_bytes=4 << 20),
        cost_estimate=cost(microseconds),
        name="heads",
    )(*arrays)


def sent_from(step):
    core, _, _ = place()
    x = lax.axis_index("tensor")
    return lax.rem(jnp.where(core == 0, x - step, x + step) + SIDE, SIDE)


def near_kernel(*refs):
    pieces, weight, keys_out, values_out, rows = refs[:3], *refs[3:]
    size = pieces[0].shape[0]
    for i, piece in enumerate(pieces):
        rows[i * size : (i + 1) * size, :] = piece[...]
    keys = jnp.zeros(keys_out.shape, F32)
    values = jnp.zeros(keys_out.shape, F32)
    step = 1024
    for i in range(0, rows.shape[1], step):
        part = slice(i, i + step)
        keys += jnp.dot(rows[:, part], weight[0, part, :], preferred_element_type=F32)
        values += jnp.dot(rows[:, part], weight[1, part, :], preferred_element_type=F32)
    keys_out[...] = keys
    values_out[...] = values


def project_near(pieces, weight):
    count = sum(piece.shape[0] for piece in pieces)
    wide = jax.ShapeDtypeStruct((count, weight.shape[2]), F32)
    return pl.pallas_call(
        near_kernel,
        out_shape=(wide, wide),
        in_specs=[VMEM] * 4,
        out_specs=(VMEM,) * 2,
        scratch_shapes=[pltpu.VMEM((count, weight.shape[1]), BF16)],
        compiler_params=pltpu.CompilerParams(vmem_limit_bytes=24 << 20),
        cost_estimate=cost(20),
        name="project_near",
    )(*pieces, weight)


def far_kernel(piece, near_keys, near_values, weight, cosine, sine, *refs):
    new_keys, new_values, mine, give = refs
    size = piece.shape[0]
    keys = jnp.zeros((size, weight.shape[2]), F32)
    values = jnp.zeros((size, weight.shape[2]), F32)
    step = 1024
    for i in range(0, piece.shape[1], step):
        part = slice(i, i + step)
        keys += jnp.dot(piece[:, part], weight[0, part, :], preferred_element_type=F32)
        values += jnp.dot(piece[:, part], weight[1, part, :], preferred_element_type=F32)
    for i, back in enumerate(ARRIVAL):
        at = pl.ds(pl.multiple_of(sent_from(back) * size, size), size)
        part = slice(i * size, (i + 1) * size)
        last = i == len(ARRIVAL) - 1
        for h in range(2):
            head = slice(h * HEAD_DIM, (h + 1) * HEAD_DIM)
            key = keys[:, head] if last else near_keys[part, head]
            turned = key * cosine[at, :] + pltpu.roll(key, HEAD_DIM // 2, 1) * sine[at, :]
            new_keys[at, head] = turned.astype(BF16)
        value = values if last else near_values[part, :]
        new_values[at, :] = value.astype(BF16)
    core, _, _ = place()
    for which, target in ((core, mine), (1 - core, give)):
        head = pl.ds(pl.multiple_of(which * HEAD_DIM, HEAD_DIM), HEAD_DIM)
        target[0:ROWS, :] = new_keys[:, head]
        target[ROWS : 2 * ROWS, :] = new_values[:, head]


def project_far(piece, near_keys, near_values, weight, cosine, sine):
    wide = jax.ShapeDtypeStruct((ROWS, 2 * HEAD_DIM), BF16)
    tall = jax.ShapeDtypeStruct((2 * ROWS, HEAD_DIM), BF16)
    return pl.pallas_call(
        far_kernel,
        out_shape=(wide, wide, tall, tall),
        in_specs=[VMEM] * 6,
        out_specs=(VMEM,) * 4,
        compiler_params=pltpu.CompilerParams(vmem_limit_bytes=24 << 20),
        cost_estimate=cost(0.1),
        name="project_far",
    )(piece, near_keys, near_values, weight, cosine, sine)


def absorb(query, turned_keys, values, state, visible=None):
    top, den, num = state
    scores = jnp.dot(query, turned_keys, preferred_element_type=F32)
    if visible is not None:
        scores = jnp.where(visible, scores, -1e30)
    raised = jnp.maximum(top, jnp.max(scores, axis=1, keepdims=True))
    weights = [
        jnp.exp2((scores[:, i : i + HEAD_DIM] - raised) * EXPONENT)
        for i in range(0, scores.shape[1], HEAD_DIM)
    ]
    keep = jnp.exp2((top - raised) * EXPONENT)
    den = den * keep + functools.reduce(lambda a, b: a + b, weights)
    rounded = jnp.concatenate([w.astype(BF16) for w in weights], 1)
    num = num * keep + jnp.dot(rounded, values, preferred_element_type=F32)
    return raised, den, num


TILE = 1024


def tiles(own_queries, received):
    found = []
    for i in range(0, SHARE * ROWS, TILE):
        found.append((0, i, functools.partial(own_queries.__getitem__, slice(i, i + TILE))))
    for i in range(0, SHARE * ROWS, TILE):
        there = slice(i, i + TILE)
        found.append((1, SHARE * ROWS + i, functools.partial(received.__getitem__, there)))
    return found


STATE = jax.ShapeDtypeStruct((2 * SHARE * ROWS, HEAD_DIM), F32)


def cache_kernel(live_keys, kv_blocks, own_queries, received, *refs):
    pieces, states, (turned, rest), (keys, values) = refs[:4], refs[4:7], refs[7:9], refs[9:]
    first = live_keys - rest.shape[0]
    core, _, _ = place()
    at = jnp.int32(0)
    for piece in range(SIDE):
        for slot in range(SIDE):
            chip = sender(piece, slot)
            for half in range(2):
                group = chip * 2 + (core if half == 0 else 1 - core)
                row = slot * 4 * ROWS + half * 2 * ROWS
                there = pl.ds(pl.multiple_of(at, BLOCK), ROWS)
                keys[there, :] = pieces[piece][row : row + ROWS, :]
                values[there, :] = pieces[piece][row + ROWS : row + 2 * ROWS, :]
                at = at + kv_blocks[group] * BLOCK
    for i in range(0, live_keys, 256):
        turned[:, i : i + 256] = keys[i : i + 256, :].T
    rest[...] = values[first:live_keys, :]
    for _, start, query in tiles(own_queries, received):
        zero = jnp.zeros((TILE, HEAD_DIM), F32)
        state = (jnp.full((TILE, HEAD_DIM), -1e30, F32), zero, zero)
        state = absorb(query(), turned[:, :first], values[:first, :], state)
        for ref, value in zip(states, state):
            ref[start : start + TILE, :] = value


def attend_cache(kv_blocks, own_queries, received, pieces, live_keys, later):
    held = pltpu.VMEM((live_keys + ROWS, HEAD_DIM), BF16)
    return pl.pallas_call(
        functools.partial(cache_kernel, live_keys),
        out_shape=(STATE,) * 3
        + (
            jax.ShapeDtypeStruct((HEAD_DIM, live_keys), BF16),
            jax.ShapeDtypeStruct((later, HEAD_DIM), BF16),
        ),
        in_specs=[SMEM] + [VMEM] * 6,
        out_specs=(VMEM,) * 5,
        scratch_shapes=[held, held],
        compiler_params=pltpu.CompilerParams(vmem_limit_bytes=24 << 20),
        cost_estimate=cost(0.1),
        name="attend_cache",
    )(kv_blocks, own_queries, received, *pieces)


def later_kernel(own_queries, received, turned, values, *refs):
    olds, states = refs[:3], refs[3:]
    first = turned.shape[1] - values.shape[0]
    for _, start, query in tiles(own_queries, received):
        rows = slice(start, start + TILE)
        state = tuple(old[rows, :] for old in olds)
        state = absorb(query(), turned[:, first:], values[...], state)
        for ref, value in zip(states, state):
            ref[rows, :] = value


def attend_later(own_queries, received, turned, values, states):
    return pl.pallas_call(
        later_kernel,
        out_shape=(STATE,) * 3,
        in_specs=[VMEM] * 7,
        out_specs=(VMEM,) * 3,
        compiler_params=pltpu.CompilerParams(vmem_limit_bytes=24 << 20),
        cost_estimate=cost(0.1),
        name="attend_later",
    )(own_queries, received, turned, values, *states)


def new_kernel(which, last, own_queries, received, *refs):
    count = len(which)
    pieces, olds = refs[:count], refs[count : count + 3]
    outs, (turned, held), sums = refs[count + 3 :], refs[-5:-3], refs[-3:]
    core, y, z = place()
    size = 2 * ROWS
    if not last:
        sums = outs[:3]
    parts = tiles(own_queries, received)

    def visit(keys, values, sources, visible=None):
        for partner, start, query in parts:
            rows = slice(start, start + TILE)
            state = absorb(
                query(),
                keys,
                values,
                tuple(s[rows, :] for s in sources),
                visible(partner) if visible else None,
            )
            for s, value in zip(sums, state):
                s[rows, :] = value

    def block_of(ref, slot):
        base = slot * 4 * ROWS
        here = [slice(base + i * ROWS, base + (i + 1) * ROWS) for i in range(4)]
        keys = jnp.concatenate([ref[here[0], :], ref[here[2], :]], 0)
        return keys.T, jnp.concatenate([ref[here[1], :], ref[here[3], :]], 0)

    def causal(partner):
        shape = (TILE, size)
        row = lax.rem(lax.broadcasted_iota(jnp.int32, shape, 0), ROWS)
        row = row + jnp.where(core == partner, 0, ROWS)
        key = lax.broadcasted_iota(jnp.int32, shape, 1)
        key = jnp.where(core == 0, key, lax.rem(key + ROWS, size))
        return key <= row

    found = jnp.int32(0)
    for piece, ref in zip(which, pieces):
        for slot in range(SIDE):
            if piece == 0 and slot == 0:
                continue
            seen = sender(piece, slot) < y * SIDE + z

            def keep(ref=ref, slot=slot, found=found):
                there = pl.ds(pl.multiple_of(found * size, size), size)
                turned[:, there], held[there, :] = block_of(ref, slot)

            pl.when(seen)(keep)
            found = found + seen.astype(jnp.int32)

    def chunk(first, blocks, sources):
        there = pl.ds(pl.multiple_of(first * size, size), blocks * size)
        visit(turned[:, there], held[there, :], sources)

    def rest(first, sources):
        left = found - first

        def body(i, _):
            chunk(first + 4 * i, 4, sources)
            return 0

        lax.fori_loop(0, left // 4, body, 0)
        pl.when((left & 2) != 0)(lambda: chunk(first + (left // 4) * 4, 2, sources))
        pl.when((left & 1) != 0)(lambda: chunk(found - 1, 1, sources))

    if which[0] == 0:
        visit(*block_of(pieces[0], 0), olds, causal)
    else:
        for new, old in zip(sums, olds):
            new[...] = old[...]
    rest(jnp.int32(0), sums)

    if last:
        here, there = outs[:2]
        for partner, target in ((0, here), (1, there)):
            for head in range(SHARE):
                start = (partner * SHARE + head) * ROWS
                rows = slice(start, start + ROWS)
                den = jnp.sum(sums[1][rows, :], axis=1, keepdims=True)
                columns = slice(head * HEAD_DIM, (head + 1) * HEAD_DIM)
                target[:, columns] = (sums[2][rows, :] / den).astype(BF16)


def attend_new(own_queries, received, which, pieces, states, last):
    out = jax.ShapeDtypeStruct((ROWS, SHARE * HEAD_DIM), BF16)
    blocks = SIDE * len(which)
    total = pltpu.VMEM(STATE.shape if last else (8, HEAD_DIM), F32)
    return pl.pallas_call(
        functools.partial(new_kernel, which, last),
        out_shape=(out, out) if last else (STATE,) * 3,
        in_specs=[VMEM] * (2 + len(which) + 3),
        out_specs=(VMEM,) * (2 if last else 3),
        scratch_shapes=[
            pltpu.VMEM((HEAD_DIM, 2 * ROWS * blocks), BF16),
            pltpu.VMEM((2 * ROWS * blocks, HEAD_DIM), BF16),
            total,
            total,
            total,
        ],
        compiler_params=pltpu.CompilerParams(vmem_limit_bytes=24 << 20),
        cost_estimate=cost(0.1),
        name="attend_new_last" if last else "attend_new",
    )(own_queries, received, *pieces, *states)


def finish_kernel(here, other, keys, values, attended, keys_out, values_out, sems):
    core, _, _ = place()
    width = here.shape[1]

    def half(i):
        return attended.at[:, pl.ds(pl.multiple_of(i * width, width), width)]

    copies = [
        pltpu.make_async_copy(source, target, sems.at[i])
        for i, (source, target) in enumerate(
            ((here, half(core)), (other, half(1 - core)), (keys, keys_out), (values, values_out))
        )
    ]
    for copy in copies:
        copy.start()
    for copy in copies:
        copy.wait()


def finish(here, other, keys, values):
    rows, width = here.shape
    hbm = pl.BlockSpec(memory_space=pltpu.HBM)
    return pl.pallas_call(
        finish_kernel,
        out_shape=tuple(
            jax.ShapeDtypeStruct(shape, BF16) for shape in ((rows, 2 * width), keys.shape, values.shape)
        ),
        in_specs=[VMEM] * 4,
        out_specs=(hbm,) * 3,
        scratch_shapes=[pltpu.SemaphoreType.DMA((4,))],
        compiler_params=pltpu.CompilerParams(vmem_limit_bytes=4 << 20),
        cost_estimate=cost(0.1),
        name="finish",
    )(here, other, keys, values)


def after(value, *others):
    return lax.optimization_barrier((value, *others))[0]


def first_phase(block, *others):
    sent = [lax.ppermute(block, "group", along(0, d)) for d in (1, 3, 2)]
    return jnp.concatenate([after(block, *others) if others else block] + sent, 0)


def second_phase(joined):
    return [joined] + [lax.ppermute(joined, "group", along(1, d)) for d in (1, 3)]


def last_phase(joined, *others):
    return lax.ppermute(after(joined, *others), "group", along(1, 2))


def swapped(block):
    return lax.ppermute(block, "group", swap_cores())


def shards(queries, hidden_rows, kv_weight, cache_keys, cache_values, kv_blocks):
    group = lax.axis_index("group")
    core = lax.rem(group, 2)
    both = ("group", "tensor")
    ahead = lax.ppermute(hidden_rows, both, ring(1))
    mine, give = heads(HEAD_DIM, 0.1, cache_keys, cache_values)
    block = jnp.concatenate([mine, swapped(give)], 0)
    behind = lax.ppermute(after(hidden_rows, block), both, ring(3))
    joined = first_phase(block)
    own_queries, give_queries = heads(SHARE * HEAD_DIM, 5, after(queries, block))
    received = swapped(give_queries)
    far = lax.ppermute(after(ahead, own_queries), both, ring(1))
    cache = second_phase(joined)

    live_keys = cache_keys.shape[0] * kv_blocks.shape[0] // 2
    half = HEAD_DIM // 2
    positions = live_keys + group * ROWS + jnp.arange(ROWS, dtype=jnp.int32)
    freq = jnp.exp(jnp.arange(half, dtype=F32) * (-2.0 * math.log(500000.0) / HEAD_DIM))
    angle = positions.astype(F32)[:, None] * freq[None, :]
    cosine, sine = jnp.cos(angle), jnp.sin(angle)
    near_keys, near_values = project_near((hidden_rows, ahead, behind), kv_weight)
    cache.append(last_phase(joined, near_keys))
    new_keys, new_values, mine, give = project_far(
        after(far, received),
        near_keys,
        near_values,
        kv_weight,
        jnp.concatenate([cosine, cosine], 1),
        jnp.concatenate([-sine, sine], 1),
    )
    block = jnp.concatenate([mine, swapped(give)], 0)
    *states, turned, values = attend_cache(
        kv_blocks, after(own_queries, block), received, cache, live_keys, live_keys // 8 * 5
    )
    joined = first_phase(block, states[0])
    new = second_phase(joined)
    states = attend_new(own_queries, received, (0,), new[:1], states, False)
    states = attend_later(own_queries, received, turned, values, states)
    new.append(last_phase(joined, states[0], new[1]))
    states = attend_new(own_queries, received, (1, 2), new[1:3], states, False)
    here, there = attend_new(own_queries, received, (3,), new[3:], states, True)
    other = swapped(there)
    return finish(here, other, new_keys, new_values)


def solution(mesh):
    placed = (
        P("group", "tensor"),
        P(("group", "tensor"), None),
        P(None, None, "tensor"),
        P("group", "tensor"),
        P("group", "tensor"),
        P(),
    )
    return jax.shard_map(
        shards,
        mesh=mesh,
        in_specs=placed,
        out_specs=(P("group", "tensor"), P("group", "tensor"), P("group", "tensor")),
        check_vma=False,
    )
```
